512 devices in a mesh: shard: 2 (over x_lo), row: 16 (over x_hi, z), col: 16 (over y, core).
Axes of the slice: x: 4 (x_hi: 2, x_lo: 2; x = x_hi * 2 + x_lo), y: 8, z: 8, core: 2. Of those that a mesh axis runs over, the one named last changes fastest.
Arguments:
- params: float32 [16, 16, 16, 5120], P('row', 'col', 'shard'), may hold values from -6 to 6
- public_copy: float32 [16, 16, 16, 5120], P('row', 'col', 'shard'), may hold values from -6 to 6
- neighbour_mix: float32 [16, 16, 16, 5120], P('row', 'col', 'shard'), may hold values from -6 to 6
- row_orders: int32 [2, 5, 1024], replicated, may hold values from 0 to 1023, each once within a row
- sign_bits: int32 [2, 5120], replicated, may hold values from 0 to 1
Outputs:
- new_params: float32 [16, 16, 16, 5120], P('row', 'col', 'shard')
- new_public: float32 [16, 16, 16, 5120], P('row', 'col', 'shard')
- new_mix: float32 [16, 16, 16, 5120], P('row', 'col', 'shard')
The draws below stay inside these ranges and needn't reach their ends.
Inputs may be any that keep to these rules, and one draw needn't show every extreme that they name: Each row of row_orders is a permutation of 0 to 1023; its first 256 entries are the kept rows.
All inputs are finite; a program needn't handle non-finite values.
Results may differ from the reference program's by a relative error of at most 0.00011.
Values sent between devices are 32-bit elements; how exact they have to be, the bound alone decides.
A program may use at most 64 MiB of HBM per device.

```python
import jax
import jax.numpy as jnp
from jax import lax

W = 5120
B = 1024
K = 256
ROUNDS = 2
NB = 5
ROWS_ALL = 16
N_ROW = 16
N_COL = 16


def place_ends(array, key, low, top_value):
    longest = array.shape.index(max(array.shape))
    spots = []
    for shift in (0, 1):
        where = [jax.random.randint(jax.random.fold_in(key, axis), (), 0, length) for axis, length in enumerate(array.shape)]
        where[longest] = (where[longest] + shift) % array.shape[longest]
        spots.append(tuple(where))
    return array.at[spots[0]].set(low).at[spots[1]].set(top_value)


def shard_levels(own_key, shape, split, smallest, top_value):
    def one(axis_at, parts):
        draws = jax.random.uniform(jax.random.fold_in(jax.random.fold_in(own_key, 6), axis_at), (parts,), jnp.float32, smallest / len(split), top_value / len(split))
        return jnp.repeat(jnp.exp(draws), shape[axis_at] // parts).reshape((-1,) + (1,) * (len(shape) - axis_at - 1))

    gain = one(*split[0])
    for cut in split[1:]:
        gain = gain * one(*cut)
    return gain


def noise(rng, shape, deviation, limit, pieces=(), dtype=jnp.bfloat16):
    result = deviation * jax.random.normal(rng, shape, jnp.float32)
    if pieces:
        result = result * shard_levels(rng, shape, pieces, -0.22, 0.18)
    return jnp.clip(result, -limit, limit).astype(dtype)


def setup_inputs(seed: int = 0) -> dict:
    keys = jax.random.split(jax.random.key(seed), 6)
    return {
        "params": noise(keys[0], (N_ROW, N_COL, ROWS_ALL, W), 1.0, 6.0, ((0, 16), (1, 16), (2, 2)), jnp.float32),
        "public_copy": noise(keys[1], (N_ROW, N_COL, ROWS_ALL, W), 1.0, 6.0, ((0, 16), (1, 16), (2, 2)), jnp.float32),
        "neighbour_mix": noise(keys[2], (N_ROW, N_COL, ROWS_ALL, W), 1.0, 6.0, ((0, 16), (1, 16), (2, 2)), jnp.float32),
        "row_orders": jax.vmap(lambda own: jax.random.permutation(own, B))(jax.random.split(keys[3], ROUNDS * NB)).reshape((ROUNDS, NB, B)).astype(jnp.int32),
        "sign_bits": place_ends(jax.random.randint(keys[4], (ROUNDS, W), 0, 2), jax.random.fold_in(keys[4], 1), 0, 1).astype(jnp.int32),
    }


mix_weight = 0.2
step_gamma = 0.5

def projection(orders, bits, keep, block):
    kept = orders[:, :keep]
    column = lax.iota(jnp.int32, block)
    value = jnp.bitwise_and(kept[:, :, None], column[None, None, :])
    value = jnp.bitwise_xor(value, jnp.right_shift(value, 16))
    value = jnp.bitwise_xor(value, jnp.right_shift(value, 8))
    value = jnp.bitwise_xor(value, jnp.right_shift(value, 4))
    value = jnp.bitwise_xor(value, jnp.right_shift(value, 2))
    value = jnp.bitwise_xor(value, jnp.right_shift(value, 1))
    parity = jnp.bitwise_and(value, 1)
    signs = (2 * bits - 1).reshape(orders.shape[0], 1, block)
    entries = (1 - 2 * parity) * signs
    return entries.astype(jnp.float32) / jnp.sqrt(jnp.float32(block))

def reference(params, public_copy, neighbour_mix, row_orders, sign_bits):
    current, public, mixed = (params, public_copy, neighbour_mix)
    shape = params.shape
    for round_index in range(ROUNDS):
        proj = projection(row_orders[round_index], sign_bits[round_index], K, B)
        diff = (current - public).reshape(shape[0], shape[1], shape[2], NB, B)
        code = jnp.einsum('xyrjb,jkb->xyrjk', diff, proj, precision=lax.Precision.HIGHEST)
        total = code + jnp.roll(code, 1, 0) + jnp.roll(code, -1, 0) + jnp.roll(code, 1, 1) + jnp.roll(code, -1, 1)
        total = mix_weight * total
        scale = jnp.float32(B / K)
        own = scale * jnp.einsum('xyrjk,jkb->xyrjb', code, proj, precision=lax.Precision.HIGHEST)
        incoming = scale * jnp.einsum('xyrjk,jkb->xyrjb', total, proj, precision=lax.Precision.HIGHEST)
        public = public + own.reshape(shape)
        mixed = mixed + incoming.reshape(shape)
        current = current + step_gamma * (mixed - public)
    return (current, public, mixed)
```

```python
import functools

import jax
import jax.numpy as jnp
from jax import lax
from jax.experimental import pallas as pl
from jax.experimental.pallas import tpu as pltpu
from jax.sharding import PartitionSpec as P

W = 5120
B = 1024
K = 256
ROUNDS = 2
NB = W // B
LANES = 128
CHUNKS = B // LANES

mix_weight = 0.2
step_gamma = 0.5
decode_scale = 1.0 / K

GROUPS = ((0, 1), (1, 2), (2, 3), (3, 4), (4, 5))

f32 = jnp.float32
bf16 = jnp.bfloat16


def plus_minus(value, bits):
    shift = bits
    while shift > 1:
        shift = (shift + 1) // 2
        value = value ^ (value >> shift)
    return (1 - 2 * (value & 1)).astype(f32)


def low_matrix(order):
    column = lax.broadcasted_iota(jnp.int32, (LANES, K), 0)
    return plus_minus((order & (LANES - 1)) & column, 8).astype(bf16)


def high_signs(order, rows):
    chunk = lax.broadcasted_iota(jnp.int32, (CHUNKS * rows, K), 0) // rows
    return plus_minus((order >> 7) & chunk, 4)


def halves(value):
    top = value.astype(bf16)
    return top, (value - top.astype(f32)).astype(bf16)


def encode(diff, low, high):
    rows = diff.shape[0]
    stacked = jnp.concatenate([diff[:, c * LANES:(c + 1) * LANES] for c in range(CHUNKS)], axis=0)
    both = jnp.concatenate(halves(stacked), axis=1)
    twice = jnp.concatenate([low, low], axis=0)
    parts = high * jnp.dot(both, twice, preferred_element_type=f32)
    return jnp.sum(parts.reshape(CHUNKS, rows, K), axis=0)


def decode(code, low, high):
    rows = code.shape[0]
    spread = high * jnp.concatenate([code] * CHUNKS, axis=0)
    both = jnp.concatenate(halves(spread), axis=0)
    result = lax.dot_general(both, low, (((1,), (1,)), ((), ())), preferred_element_type=f32)
    result = result[:CHUNKS * rows] + result[CHUNKS * rows:]
    return jnp.concatenate([result[c * rows:(c + 1) * rows] for c in range(CHUNKS)], axis=1)


def kernel(n_row, n_col, x_in, h_in, s_in, order_in, bits_in, x_out, h_out, s_out,
           x_v, h_v, s_v, u_v, order_v, bits_v, low_v, high_v, code_v, got_v,
           in_sem, out_sem, send_sem, recv_sem):
    rows = x_v.shape[0]
    row, col = lax.axis_index("row"), lax.axis_index("col")
    neighbours = (
        {"row": lax.rem(row + 1, n_row)},
        {"row": lax.rem(row + n_row - 1, n_row)},
        {"col": lax.rem(col + 1, n_col)},
        {"col": lax.rem(col + n_col - 1, n_col)},
    )

    loads = [
        pltpu.make_async_copy(order_in.at[:, :, pl.ds(0, K)], order_v, in_sem.at[0]),
        pltpu.make_async_copy(bits_in, bits_v, in_sem.at[1]),
        pltpu.make_async_copy(x_in.at[0, 0], x_v, in_sem.at[2]),
        pltpu.make_async_copy(h_in.at[0, 0], h_v, in_sem.at[3]),
        pltpu.make_async_copy(s_in.at[0, 0], s_v, in_sem.at[4]),
    ]
    for load in loads:
        load.start()

    barrier = pltpu.get_barrier_semaphore()
    for neighbour in neighbours:
        pl.semaphore_signal(barrier, inc=1, device_id=neighbour, device_id_type=pl.DeviceIdType.MESH)

    def build(r):
        for j in range(NB):
            order = order_v[r, j:j + 1, :]
            low_v[r, j] = low_matrix(order)
            high_v[r, j] = high_signs(order, rows)

    def columns(j):
        return slice(j * B, (j + 1) * B)

    def sign(r, j):
        return (2 * bits_v[r:r + 1, columns(j)] - 1).astype(f32)

    copies = {}

    def send(r, g):
        first, last = GROUPS[g]
        part = pl.ds(first, last - first)
        for n, neighbour in enumerate(neighbours):
            copy = pltpu.make_async_remote_copy(
                src_ref=code_v.at[r, part],
                dst_ref=got_v.at[r, n, part],
                send_sem=send_sem.at[r, g, n],
                recv_sem=recv_sem.at[r, g, n],
                device_id=neighbour,
                device_id_type=pl.DeviceIdType.MESH,
            )
            copy.start()
            copies[r, g, n] = copy

    def incoming(r, j):
        total = code_v[r, j] + got_v[r, 0, j] + got_v[r, 1, j] + got_v[r, 2, j] + got_v[r, 3, j]
        return sign(r, j) * decode((mix_weight * decode_scale) * total, low_v[r, j], high_v[r, j])

    def own(r, j):
        return sign(r, j) * decode(decode_scale * code_v[r, j], low_v[r, j], high_v[r, j])

    loads[0].wait()
    build(0)
    for load in loads[1:4]:
        load.wait()
    for g, (first, last) in enumerate(GROUPS):
        for j in range(first, last):
            diff = sign(0, j) * (x_v[:, columns(j)] - h_v[:, columns(j)])
            code_v[0, j] = encode(diff, low_v[0, j], high_v[0, j])
        if g == 0:
            pl.semaphore_wait(barrier, 4)
        send(0, g)

    build(1)
    loads[4].wait()
    for j in range(NB):
        cols = columns(j)
        public = h_v[:, cols] + own(0, j)
        h_v[:, cols] = public
        u_v[:, cols] = x_v[:, cols] + step_gamma * s_v[:, cols] - (1 + step_gamma) * public

    for g, (first, last) in enumerate(GROUPS):
        for n in range(4):
            copies[0, g, n].wait_recv()
        for j in range(first, last):
            cols = columns(j)
            update = incoming(0, j)
            s_v[:, cols] = s_v[:, cols] + update
            diff = sign(1, j) * (u_v[:, cols] + step_gamma * update)
            code_v[1, j] = encode(diff, low_v[1, j], high_v[1, j])
        send(1, g)

    for j in range(NB):
        cols = columns(j)
        before = h_v[:, cols]
        public = before + own(1, j)
        h_v[:, cols] = public
        mixed = s_v[:, cols]
        x_v[:, cols] = x_v[:, cols] + step_gamma * (mixed - before) + step_gamma * (mixed - public)
    stores = [pltpu.make_async_copy(h_v, h_out.at[0, 0], out_sem.at[0])]
    stores[0].start()

    for g, (first, last) in enumerate(GROUPS):
        for n in range(4):
            copies[1, g, n].wait_recv()
        for j in range(first, last):
            cols = columns(j)
            update = incoming(1, j)
            s_v[:, cols] = s_v[:, cols] + update
            x_v[:, cols] = x_v[:, cols] + step_gamma * update
    stores.append(pltpu.make_async_copy(x_v, x_out.at[0, 0], out_sem.at[1]))
    stores.append(pltpu.make_async_copy(s_v, s_out.at[0, 0], out_sem.at[2]))
    for store in stores[1:]:
        store.start()
    for copy in copies.values():
        copy.wait_send()
    for store in stores:
        store.wait()


def local(n_row, n_col, params, public_copy, neighbour_mix, row_orders, sign_bits):
    rows = params.shape[2]
    anywhere = pl.BlockSpec(memory_space=pl.ANY)
    shape = jax.ShapeDtypeStruct(params.shape, f32)
    whole = pltpu.VMEM((rows, W), f32)
    return pl.pallas_call(
        functools.partial(kernel, n_row, n_col),
        out_shape=(shape, shape, shape),
        in_specs=[anywhere] * 5,
        out_specs=(anywhere, anywhere, anywhere),
        scratch_shapes=[
            whole, whole, whole, whole,
            pltpu.VMEM((ROUNDS, NB, K), jnp.int32),
            pltpu.VMEM((ROUNDS, W), jnp.int32),
            pltpu.VMEM((ROUNDS, NB, LANES, K), bf16),
            pltpu.VMEM((ROUNDS, NB, CHUNKS * rows, K), f32),
            pltpu.VMEM((ROUNDS, NB, rows, K), f32),
            pltpu.VMEM((ROUNDS, 4, NB, rows, K), f32),
            pltpu.SemaphoreType.DMA((5,)),
            pltpu.SemaphoreType.DMA((3,)),
            pltpu.SemaphoreType.DMA((ROUNDS, len(GROUPS), 4)),
            pltpu.SemaphoreType.DMA((ROUNDS, len(GROUPS), 4)),
        ],
        compiler_params=pltpu.CompilerParams(
            collective_id=0, has_side_effects=True, vmem_limit_bytes=32 * 1024 * 1024
        ),
    )(params, public_copy, neighbour_mix, row_orders, sign_bits)


def solution(mesh):
    split = P("row", "col", "shard", None)
    return jax.shard_map(
        functools.partial(local, mesh.shape["row"], mesh.shape["col"]),
        mesh=mesh,
        in_specs=(split, split, split, P(), P()),
        out_specs=(split, split, split),
        check_vma=False,
    )
```

```python
import functools

import jax
import jax.numpy as jnp
from jax import lax
from jax.experimental import pallas as pl
from jax.experimental.pallas import tpu as pltpu
from jax.sharding import PartitionSpec as P

W = 5120
B = 1024
K = 256
ROUNDS = 2
NB = W // B
LANES = 128
CHUNKS = B // LANES

mix_weight = 0.2
step_gamma = 0.5
decode_scale = 1.0 / K

GROUPS = ((0, 5),)

f32 = jnp.float32
bf16 = jnp.bfloat16


def plus_minus(value, bits):
    shift = bits
    while shift > 1:
        shift = (shift + 1) // 2
        value = value ^ (value >> shift)
    return (1 - 2 * (value & 1)).astype(f32)


def low_matrix(order):
    column = lax.broadcasted_iota(jnp.int32, (LANES, K), 0)
    return plus_minus((order & (LANES - 1)) & column, 8).astype(bf16)


def high_signs(order, rows):
    chunk = lax.broadcasted_iota(jnp.int32, (CHUNKS * rows, K), 0) // rows
    return plus_minus((order >> 7) & chunk, 4)


def halves(value):
    top = value.astype(bf16)
    return top, (value - top.astype(f32)).astype(bf16)


def encode(diff, low, high):
    rows = diff.shape[0]
    stacked = jnp.concatenate([diff[:, c * LANES:(c + 1) * LANES] for c in range(CHUNKS)], axis=0)
    both = jnp.concatenate(halves(stacked), axis=1)
    twice = jnp.concatenate([low, low], axis=0)
    parts = high * jnp.dot(both, twice, preferred_element_type=f32)
    return jnp.sum(parts.reshape(CHUNKS, rows, K), axis=0)


def decode(code, low, high):
    rows = code.shape[0]
    spread = high * jnp.concatenate([code] * CHUNKS, axis=0)
    both = jnp.concatenate(halves(spread), axis=0)
    result = lax.dot_general(both, low, (((1,), (1,)), ((), ())), preferred_element_type=f32)
    result = result[:CHUNKS * rows] + result[CHUNKS * rows:]
    return jnp.concatenate([result[c * rows:(c + 1) * rows] for c in range(CHUNKS)], axis=1)


def kernel(n_row, n_col, x_in, h_in, s_in, order_in, bits_in, x_v, h_v, s_v,
           u_v, order_v, bits_v, low_v, high_v, code_v, got_v,
           in_sem, send_sem, recv_sem):
    rows = x_v.shape[0]
    row, col = lax.axis_index("row"), lax.axis_index("col")
    neighbours = (
        {"row": lax.rem(row + 1, n_row)},
        {"row": lax.rem(row + n_row - 1, n_row)},
        {"col": lax.rem(col + 1, n_col)},
        {"col": lax.rem(col + n_col - 1, n_col)},
    )

    loads = [
        pltpu.make_async_copy(order_in.at[:, :, pl.ds(0, K)], order_v, in_sem.at[0]),
        pltpu.make_async_copy(bits_in, bits_v, in_sem.at[1]),
        pltpu.make_async_copy(x_in.at[0, 0], x_v, in_sem.at[2]),
        pltpu.make_async_copy(h_in.at[0, 0], h_v, in_sem.at[3]),
        pltpu.make_async_copy(s_in.at[0, 0], s_v, in_sem.at[4]),
    ]
    for load in loads:
        load.start()

    barrier = pltpu.get_barrier_semaphore()
    for neighbour in neighbours:
        pl.semaphore_signal(barrier, inc=1, device_id=neighbour, device_id_type=pl.DeviceIdType.MESH)

    def build(r):
        for j in range(NB):
            order = order_v[j, r:r + 1, :]
            low_v[r, j] = low_matrix(order)
            high_v[r, j] = high_signs(order, rows)

    def columns(j):
        return slice(j * B, (j + 1) * B)

    def sign(r, j):
        return (2 * bits_v[r:r + 1, columns(j)] - 1).astype(f32)

    copies = {}

    def send(r, g):
        first, last = GROUPS[g]
        part = pl.ds(first, last - first)
        for n, neighbour in enumerate(neighbours):
            copy = pltpu.make_async_remote_copy(
                src_ref=code_v.at[r, part],
                dst_ref=got_v.at[r, n, part],
                send_sem=send_sem.at[r, g, n],
                recv_sem=recv_sem.at[r, g, n],
                device_id=neighbour,
                device_id_type=pl.DeviceIdType.MESH,
            )
            copy.start()
            copies[r, g, n] = copy

    def incoming(r, j):
        total = code_v[r, j] + got_v[r, 0, j] + got_v[r, 1, j] + got_v[r, 2, j] + got_v[r, 3, j]
        return sign(r, j) * decode((mix_weight * decode_scale) * total, low_v[r, j], high_v[r, j])

    def own(r, j):
        return sign(r, j) * decode(decode_scale * code_v[r, j], low_v[r, j], high_v[r, j])

    loads[0].wait()
    build(0)
    for load in loads[1:4]:
        load.wait()
    for g, (first, last) in enumerate(GROUPS):
        for j in range(first, last):
            diff = sign(0, j) * (x_v[:, columns(j)] - h_v[:, columns(j)])
            code_v[0, j] = encode(diff, low_v[0, j], high_v[0, j])
        if g == 0:
            pl.semaphore_wait(barrier, 4)
        send(0, g)

    build(1)
    loads[4].wait()
    for j in range(NB):
        cols = columns(j)
        public = h_v[:, cols] + own(0, j)
        h_v[:, cols] = public
        u_v[:, cols] = x_v[:, cols] + step_gamma * s_v[:, cols] - (1 + step_gamma) * public

    for g, (first, last) in enumerate(GROUPS):
        for n in range(4):
            copies[0, g, n].wait_recv()
        for j in range(first, last):
            cols = columns(j)
            update = incoming(0, j)
            s_v[:, cols] = s_v[:, cols] + update
            diff = sign(1, j) * (u_v[:, cols] + step_gamma * update)
            code_v[1, j] = encode(diff, low_v[1, j], high_v[1, j])
        send(1, g)

    for j in range(NB):
        cols = columns(j)
        before = h_v[:, cols]
        public = before + own(1, j)
        h_v[:, cols] = public
        mixed = s_v[:, cols]
        x_v[:, cols] = x_v[:, cols] + step_gamma * (mixed - before) + step_gamma * (mixed - public)

    for g, (first, last) in enumerate(GROUPS):
        for n in range(4):
            copies[1, g, n].wait_recv()
        for j in range(first, last):
            cols = columns(j)
            update = incoming(1, j)
            s_v[:, cols] = s_v[:, cols] + update
            x_v[:, cols] = x_v[:, cols] + step_gamma * update
    for copy in copies.values():
        copy.wait_send()


def store_kernel(x_in, h_in, s_in, x_out, h_out, s_out, sem):
    pairs = ((x_in, x_out), (h_in, h_out), (s_in, s_out))
    copies = [pltpu.make_async_copy(a, b.at[0, 0], sem.at[i]) for i, (a, b) in enumerate(pairs)]
    for copy in copies:
        copy.start()
    for copy in copies:
        copy.wait()


def local(n_row, n_col, params, public_copy, neighbour_mix, row_orders, sign_bits):
    rows = params.shape[2]
    hbm = pl.BlockSpec(memory_space=pltpu.HBM)
    vmem = pl.BlockSpec(memory_space=pltpu.VMEM)
    shape = jax.ShapeDtypeStruct(params.shape, f32)
    flat = pltpu.VMEM((rows, W), f32)
    whole = pltpu.VMEM((rows, W), f32)
    results = pl.pallas_call(
        functools.partial(kernel, n_row, n_col),
        out_shape=(flat, flat, flat),
        in_specs=[hbm] * 5,
        out_specs=(vmem, vmem, vmem),
        scratch_shapes=[
            whole,
            pltpu.VMEM((NB, ROUNDS, K), jnp.int32),
            pltpu.VMEM((ROUNDS, W), jnp.int32),
            pltpu.VMEM((ROUNDS, NB, LANES, K), bf16),
            pltpu.VMEM((ROUNDS, NB, CHUNKS * rows, K), f32),
            pltpu.VMEM((ROUNDS, NB, rows, K), f32),
            pltpu.VMEM((ROUNDS, 4, NB, rows, K), f32),
            pltpu.SemaphoreType.DMA((5,)),
            pltpu.SemaphoreType.DMA((ROUNDS, len(GROUPS), 4)),
            pltpu.SemaphoreType.DMA((ROUNDS, len(GROUPS), 4)),
        ],
        compiler_params=pltpu.CompilerParams(
            collective_id=0, has_side_effects=True, vmem_limit_bytes=32 * 1024 * 1024
        ),
    )(*(pltpu.with_memory_space_constraint(a, pltpu.HBM) for a in (
        params, public_copy, neighbour_mix, jnp.transpose(row_orders, (1, 0, 2)), sign_bits)))
    return pl.pallas_call(
        store_kernel,
        out_shape=(shape, shape, shape),
        in_specs=[vmem] * 3,
        out_specs=(hbm, hbm, hbm),
        scratch_shapes=[pltpu.SemaphoreType.DMA((3,))],
    )(*(pltpu.with_memory_space_constraint(a, pltpu.VMEM) for a in results))


def solution(mesh):
    split = P("row", "col", "shard", None)
    return jax.shard_map(
        functools.partial(local, mesh.shape["row"], mesh.shape["col"]),
        mesh=mesh,
        in_specs=(split, split, split, P(), P()),
        out_specs=(split, split, split),
        check_vma=False,
    )
```

```python
import functools

import jax
import jax.numpy as jnp
from jax import lax
from jax.experimental import pallas as pl
from jax.experimental.pallas import tpu as pltpu
from jax.sharding import PartitionSpec as P

W = 5120
B = 1024
K = 256
ROUNDS = 2
NB = W // B
LANES = 128
CHUNKS = B // LANES

mix_weight = 0.2
step_gamma = 0.5
decode_scale = 1.0 / K

EDGE = 8
NEXT_ROW, PREV_ROW, NEXT_COL, PREV_COL = range(4)

f32 = jnp.float32
bf16 = jnp.bfloat16


def plus_minus(value, bits):
    shift = bits
    while shift > 1:
        shift = (shift + 1) // 2
        value = value ^ (value >> shift)
    return (1 - 2 * (value & 1)).astype(f32)


def low_matrix(order):
    column = lax.broadcasted_iota(jnp.int32, (LANES, K), 0)
    return plus_minus((order & (LANES - 1)) & column, 8).astype(bf16)


def high_signs(order, rows):
    chunk = lax.broadcasted_iota(jnp.int32, (CHUNKS * rows, K), 0) // rows
    return plus_minus((order >> 7) & chunk, 4)


def halves(value):
    top = value.astype(bf16)
    return top, (value - top.astype(f32)).astype(bf16)


def encode(diff, low, high):
    rows = diff.shape[0]
    stacked = jnp.concatenate([diff[:, c * LANES:(c + 1) * LANES] for c in range(CHUNKS)], axis=0)
    both = jnp.concatenate(halves(stacked), axis=1)
    twice = jnp.concatenate([low, low], axis=0)
    parts = high * jnp.dot(both, twice, preferred_element_type=f32)
    return jnp.sum(parts.reshape(CHUNKS, rows, K), axis=0)


def decode(code, low, high):
    rows = code.shape[0]
    spread = high * jnp.concatenate([code] * CHUNKS, axis=0)
    both = jnp.concatenate(halves(spread), axis=0)
    result = lax.dot_general(both, low, (((1,), (1,)), ((), ())), preferred_element_type=f32)
    result = result[:CHUNKS * rows] + result[CHUNKS * rows:]
    return jnp.concatenate([result[c * rows:(c + 1) * rows] for c in range(CHUNKS)], axis=1)


def kernel(n_row, n_col, x_in, h_in, s_in, order_in, bits_in, x_v, h_v, s_v,
           order_v, bits_v, low_v, high_v, code_v, first_v, self_v, got_v,
           in_sem, send_sem, recv_sem):
    rows = x_v.shape[0]
    row, col = lax.axis_index("row"), lax.axis_index("col")
    neighbours = (
        {"row": lax.rem(row + 1, n_row)},
        {"row": lax.rem(row + n_row - 1, n_row)},
        {"col": lax.rem(col + 1, n_col)},
        {"col": lax.rem(col + n_col - 1, n_col)},
    )

    loads = [
        pltpu.make_async_copy(order_in.at[:, :, pl.ds(0, K)], order_v, in_sem.at[0]),
        pltpu.make_async_copy(bits_in, bits_v, in_sem.at[1]),
        pltpu.make_async_copy(x_in.at[0, 0], x_v, in_sem.at[2]),
        pltpu.make_async_copy(h_in.at[0, 0], h_v, in_sem.at[3]),
        pltpu.make_async_copy(s_in.at[0, 0], s_v, in_sem.at[4]),
    ]
    barrier = pltpu.get_barrier_semaphore()
    for neighbour in neighbours:
        pl.semaphore_signal(barrier, inc=1, device_id=neighbour, device_id_type=pl.DeviceIdType.MESH)
    for load in loads:
        load.start()

    def build(r):
        for j in range(NB):
            order = order_v[j, r:r + 1, :]
            low_v[r, j] = low_matrix(order)
            high_v[r, j] = high_signs(order, rows)

    def columns(j):
        return slice(j * B, (j + 1) * B)

    def sign(r, j):
        return (2 * bits_v[r:r + 1, columns(j)] - 1).astype(f32)

    def copy(r, n, source):
        return pltpu.make_async_remote_copy(
            src_ref=source,
            dst_ref=got_v.at[r, n],
            send_sem=send_sem.at[r, n],
            recv_sem=recv_sem.at[r, n],
            device_id=neighbours[n],
            device_id_type=pl.DeviceIdType.MESH,
        )

    def send(r, targets, source):
        for n in targets:
            copy(r, n, source).start()

    def receive(r, sources):
        for n in sources:
            pltpu.make_async_copy(got_v.at[r, n], got_v.at[r, n], recv_sem.at[r, n]).wait()

    def spread(r, j, code):
        return sign(r, j) * decode(decode_scale * code, low_v[r, j], high_v[r, j])

    def later(j, update):
        return encode(sign(1, j) * update, low_v[1, j], high_v[1, j])

    loads[0].wait()
    build(0)
    for load in loads[1:4]:
        load.wait()
    for j in range(NB):
        cols = columns(j)
        code_v[0, j] = encode(sign(0, j) * (x_v[:, cols] - h_v[:, cols]), low_v[0, j], high_v[0, j])
    pl.semaphore_wait(barrier, 4)
    send(0, (NEXT_COL, PREV_COL, NEXT_ROW, PREV_ROW), code_v.at[0])

    build(1)
    loads[4].wait()
    for j in range(NB):
        cols = columns(j)
        update = spread(0, j, code_v[0, j])
        public = h_v[:, cols] + update
        share = mix_weight * update
        mixed = s_v[:, cols]
        x_v[:, cols] = x_v[:, cols] - step_gamma * public
        base = x_v[:, cols] + step_gamma * mixed - public
        h_v[:, cols] = public
        s_v[:, cols] = mixed + share
        self_v[j] = later(j, step_gamma * share)
        first_v[j] = later(j, base) + self_v[j]

    edge = lax.rem(row, EDGE) == 0
    early = jnp.where(edge, PREV_ROW, NEXT_ROW)
    late = jnp.where(edge, NEXT_ROW, PREV_ROW)
    receive(0, (early, NEXT_COL, PREV_COL))
    for j in range(NB):
        cols = columns(j)
        update = spread(0, j, mix_weight * (got_v[0, early, j] + got_v[0, NEXT_COL, j] + got_v[0, PREV_COL, j]))
        s_v[:, cols] = s_v[:, cols] + update
        first_v[j] = first_v[j] + later(j, step_gamma * update)

    @pl.when(jnp.logical_not(edge))
    def _():
        send(1, (NEXT_ROW,), first_v)

    receive(0, (late,))
    for j in range(NB):
        cols = columns(j)
        update = spread(0, j, mix_weight * got_v[0, late, j])
        s_v[:, cols] = s_v[:, cols] + update
        code_v[1, j] = first_v[j] + later(j, step_gamma * update)
    send(1, (NEXT_COL, PREV_COL, PREV_ROW), code_v.at[1])

    @pl.when(edge)
    def _():
        send(1, (NEXT_ROW,), code_v.at[1])

    for j in range(NB):
        cols = columns(j)
        public = h_v[:, cols] + spread(1, j, code_v[1, j])
        h_v[:, cols] = public
        x_v[:, cols] = x_v[:, cols] + step_gamma * (2 * s_v[:, cols] - public)

    left_out = jnp.where(lax.rem(row, EDGE) == 1, 0.0, 1.0)
    receive(1, range(4))
    for j in range(NB):
        cols = columns(j)
        total = code_v[1, j] + left_out * self_v[j]
        for n in range(4):
            total = total + got_v[1, n, j]
        update = spread(1, j, mix_weight * total)
        s_v[:, cols] = s_v[:, cols] + update
        x_v[:, cols] = x_v[:, cols] + step_gamma * update
    for r in range(ROUNDS):
        for n in range(4):
            copy(r, n, code_v.at[r]).wait_send()


def store_kernel(x_in, h_in, s_in, x_out, h_out, s_out, sem):
    pairs = ((x_in, x_out), (h_in, h_out), (s_in, s_out))
    copies = [pltpu.make_async_copy(a, b.at[0, 0], sem.at[i]) for i, (a, b) in enumerate(pairs)]
    for copy in copies:
        copy.start()
    for copy in copies:
        copy.wait()


def local(n_row, n_col, params, public_copy, neighbour_mix, row_orders, sign_bits):
    rows = params.shape[2]
    hbm = pl.BlockSpec(memory_space=pltpu.HBM)
    vmem = pl.BlockSpec(memory_space=pltpu.VMEM)
    shape = jax.ShapeDtypeStruct(params.shape, f32)
    flat = pltpu.VMEM((rows, W), f32)
    results = pl.pallas_call(
        functools.partial(kernel, n_row, n_col),
        out_shape=(flat, flat, flat),
        in_specs=[hbm] * 5,
        out_specs=(vmem, vmem, vmem),
        scratch_shapes=[
            pltpu.VMEM((NB, ROUNDS, K), jnp.int32),
            pltpu.VMEM((ROUNDS, W), jnp.int32),
            pltpu.VMEM((ROUNDS, NB, LANES, K), bf16),
            pltpu.VMEM((ROUNDS, NB, CHUNKS * rows, K), f32),
            pltpu.VMEM((ROUNDS, NB, rows, K), f32),
            pltpu.VMEM((NB, rows, K), f32),
            pltpu.VMEM((NB, rows, K), f32),
            pltpu.VMEM((ROUNDS, 4, NB, rows, K), f32),
            pltpu.SemaphoreType.DMA((5,)),
            pltpu.SemaphoreType.DMA((ROUNDS, 4)),
            pltpu.SemaphoreType.DMA((ROUNDS, 4)),
        ],
        compiler_params=pltpu.CompilerParams(
            collective_id=0, has_side_effects=True, vmem_limit_bytes=32 * 1024 * 1024
        ),
    )(*(pltpu.with_memory_space_constraint(a, pltpu.HBM) for a in (
        params, public_copy, neighbour_mix, jnp.transpose(row_orders, (1, 0, 2)), sign_bits)))
    return pl.pallas_call(
        store_kernel,
        out_shape=(shape, shape, shape),
        in_specs=[vmem] * 3,
        out_specs=(hbm, hbm, hbm),
        scratch_shapes=[pltpu.SemaphoreType.DMA((3,))],
    )(*(pltpu.with_memory_space_constraint(a, pltpu.VMEM) for a in results))


def solution(mesh):
    split = P("row", "col", "shard", None)
    return jax.shard_map(
        functools.partial(local, mesh.shape["row"], mesh.shape["col"]),
        mesh=mesh,
        in_specs=(split, split, split, P(), P()),
        out_specs=(split, split, split),
        check_vma=False,
    )
```

```python
import functools

import jax
import jax.numpy as jnp
from jax import lax
from jax.experimental import pallas as pl
from jax.experimental.pallas import tpu as pltpu
from jax.sharding import PartitionSpec as P

W = 5120
B = 1024
K = 256
ROUNDS = 2
NB = W // B
LANES = 128
CHUNKS = B // LANES

mix_weight = 0.2
step_gamma = 0.5
decode_scale = 1.0 / K

EDGE = 8
NEXT_ROW, PREV_ROW, NEXT_COL, PREV_COL = range(4)

f32 = jnp.float32
bf16 = jnp.bfloat16


def plus_minus(value, bits):
    shift = bits
    while shift > 1:
        shift = (shift + 1) // 2
        value = value ^ (value >> shift)
    return (1 - 2 * (value & 1)).astype(f32)


def low_matrix(order):
    column = lax.broadcasted_iota(jnp.int32, (LANES, K), 0)
    return plus_minus((order & (LANES - 1)) & column, 8).astype(bf16)


def high_signs(order, rows):
    chunk = lax.broadcasted_iota(jnp.int32, (CHUNKS * rows, K), 0) // rows
    return plus_minus((order >> 7) & chunk, 4)


def halves(value):
    top = value.astype(bf16)
    return top, (value - top.astype(f32)).astype(bf16)


def encode(diff, low, high):
    rows = diff.shape[0]
    stacked = jnp.concatenate([diff[:, c * LANES:(c + 1) * LANES] for c in range(CHUNKS)], axis=0)
    both = jnp.concatenate(halves(stacked), axis=1)
    twice = jnp.concatenate([low, low], axis=0)
    parts = high * jnp.dot(both, twice, preferred_element_type=f32)
    return jnp.sum(parts.reshape(CHUNKS, rows, K), axis=0)


def decode(code, low, high):
    rows = code.shape[0]
    spread = high * jnp.concatenate([code] * CHUNKS, axis=0)
    both = jnp.concatenate(halves(spread), axis=0)
    result = lax.dot_general(both, low, (((1,), (1,)), ((), ())), preferred_element_type=f32)
    result = result[:CHUNKS * rows] + result[CHUNKS * rows:]
    return jnp.concatenate([result[c * rows:(c + 1) * rows] for c in range(CHUNKS)], axis=1)


def kernel(n_row, n_col, x_in, h_in, s_in, order_in, bits_in, x_v, h_v, s_v,
           order_v, bits_v, low_v, high_v, code_v, got_v,
           self_v, base_v, rows_v, cols_v, next_v, last_v, side_v, both_v, full_v,
           in_sem, send_sem, recv_sem):
    rows = x_v.shape[0]
    row, col = lax.axis_index("row"), lax.axis_index("col")
    neighbours = (
        {"row": lax.rem(row + 1, n_row)},
        {"row": lax.rem(row + n_row - 1, n_row)},
        {"col": lax.rem(col + 1, n_col)},
        {"col": lax.rem(col + n_col - 1, n_col)},
    )

    loads = [
        pltpu.make_async_copy(order_in.at[:, :, pl.ds(0, K)], order_v, in_sem.at[0]),
        pltpu.make_async_copy(bits_in, bits_v, in_sem.at[1]),
        pltpu.make_async_copy(x_in.at[0, 0], x_v, in_sem.at[2]),
        pltpu.make_async_copy(h_in.at[0, 0], h_v, in_sem.at[3]),
        pltpu.make_async_copy(s_in.at[0, 0], s_v, in_sem.at[4]),
    ]
    edge = lax.rem(row, EDGE) == 0
    inner = jnp.logical_not(edge)
    before_edge = lax.rem(row, EDGE) == EDGE - 1
    even = lax.rem(col, 2) == 0
    odd = jnp.logical_not(even)
    early = jnp.where(edge, PREV_ROW, NEXT_ROW)
    late = jnp.where(edge, NEXT_ROW, PREV_ROW)

    barrier = pltpu.get_barrier_semaphore()

    def greet(n):
        pl.semaphore_signal(barrier, inc=1, device_id=neighbours[n], device_id_type=pl.DeviceIdType.MESH)

    greet(NEXT_COL)
    greet(PREV_COL)
    greet(PREV_ROW)
    pl.when(jnp.logical_not(before_edge))(lambda: greet(NEXT_ROW))
    for load in loads:
        load.start()

    def build(r):
        for j in range(NB):
            order = order_v[j, r:r + 1, :]
            low_v[r, j] = low_matrix(order)
            high_v[r, j] = high_signs(order, rows)

    def columns(j):
        return slice(j * B, (j + 1) * B)

    def sign(r, j):
        return (2 * bits_v[r:r + 1, columns(j)] - 1).astype(f32)

    def copy(r, n, source):
        return pltpu.make_async_remote_copy(
            src_ref=source,
            dst_ref=got_v.at[r, n],
            send_sem=send_sem.at[r, n],
            recv_sem=recv_sem.at[r, n],
            device_id=neighbours[n],
            device_id_type=pl.DeviceIdType.MESH,
        )

    def send(r, targets, source):
        for n in targets:
            copy(r, n, source).start()

    def receive(r, sources):
        for n in sources:
            pltpu.make_async_copy(got_v.at[r, n], got_v.at[r, n], recv_sem.at[r, n]).wait()

    def spread(r, j, code):
        return sign(r, j) * decode(decode_scale * code, low_v[r, j], high_v[r, j])

    def later(j, update):
        return encode(sign(1, j) * update, low_v[1, j], high_v[1, j])

    loads[0].wait()
    build(0)
    for load in loads[1:4]:
        load.wait()
    for j in range(NB):
        cols = columns(j)
        code_v[0, j] = encode(sign(0, j) * (x_v[:, cols] - h_v[:, cols]), low_v[0, j], high_v[0, j])
    pl.semaphore_wait(barrier, jnp.where(edge, 3, 4))
    send(0, (NEXT_COL, PREV_COL, NEXT_ROW), code_v.at[0])
    pl.when(inner)(lambda: send(0, (PREV_ROW,), code_v.at[0]))

    build(1)
    loads[4].wait()
    for j in range(NB):
        cols = columns(j)
        update = spread(0, j, code_v[0, j])
        public = h_v[:, cols] + update
        share = mix_weight * update
        mixed = s_v[:, cols]
        x_v[:, cols] = x_v[:, cols] - step_gamma * public
        base = x_v[:, cols] + step_gamma * mixed - public
        h_v[:, cols] = public
        s_v[:, cols] = mixed + share
        self_v[j] = later(j, step_gamma * share)
        base_v[j] = later(j, base) + self_v[j]

    twice = jnp.where(even, 0.0, 2.0)

    def part(j, code):
        cols = columns(j)
        update = spread(0, j, mix_weight * code)
        s_v[:, cols] = s_v[:, cols] + update
        return later(j, step_gamma * update)

    receive(0, (early,))
    for j in range(NB):
        rows_v[j] = part(j, got_v[0, early, j])
        next_v[j] = base_v[j] + rows_v[j]
    pl.when(jnp.logical_and(inner, even))(lambda: send(1, (NEXT_ROW,), next_v))

    receive(0, (NEXT_COL, PREV_COL))
    for j in range(NB):
        cols_v[j] = part(j, got_v[0, NEXT_COL, j] + got_v[0, PREV_COL, j])
        last_v[j] = base_v[j] + rows_v[j] + twice * cols_v[j]
        side_v[j] = base_v[j] + cols_v[j]
    pl.when(jnp.logical_and(inner, odd))(lambda: send(1, (NEXT_ROW,), last_v))
    pl.when(even)(lambda: send(1, (NEXT_COL, PREV_COL), side_v))

    receive(0, (late,))
    pl.when(edge)(lambda: send(0, (PREV_ROW,), code_v.at[0]))
    for j in range(NB):
        late_part = part(j, got_v[0, late, j])
        rows_v[j] = rows_v[j] + late_part
        code_v[1, j] = last_v[j] + late_part
        both_v[j] = side_v[j] + twice * rows_v[j]
    pl.when(odd)(lambda: send(1, (NEXT_COL, PREV_COL), both_v))
    pl.when(edge)(lambda: send(1, (NEXT_ROW,), code_v.at[1]))
    send(1, (PREV_ROW,), code_v.at[1])

    for j in range(NB):
        cols = columns(j)
        own = base_v[j] + rows_v[j] + cols_v[j]
        full_v[j] = own
        public = h_v[:, cols] + spread(1, j, own)
        h_v[:, cols] = public
        x_v[:, cols] = x_v[:, cols] + step_gamma * (2 * s_v[:, cols] - public)

    left_out = jnp.where(lax.rem(row, EDGE) == 1, 0.0, 1.0)
    receive(1, range(4))
    for j in range(NB):
        cols = columns(j)
        total = full_v[j] + left_out * self_v[j]
        for n in range(4):
            total = total + got_v[1, n, j]
        update = spread(1, j, mix_weight * total)
        s_v[:, cols] = s_v[:, cols] + update
        x_v[:, cols] = x_v[:, cols] + step_gamma * update
    for r in range(ROUNDS):
        for n in range(4):
            copy(r, n, code_v.at[r]).wait_send()


def store_kernel(x_in, h_in, s_in, x_out, h_out, s_out, sem):
    pairs = ((x_in, x_out), (h_in, h_out), (s_in, s_out))
    copies = [pltpu.make_async_copy(a, b.at[0, 0], sem.at[i]) for i, (a, b) in enumerate(pairs)]
    for copy in copies:
        copy.start()
    for copy in copies:
        copy.wait()


def local(n_row, n_col, params, public_copy, neighbour_mix, row_orders, sign_bits):
    rows = params.shape[2]
    hbm = pl.BlockSpec(memory_space=pltpu.HBM)
    vmem = pl.BlockSpec(memory_space=pltpu.VMEM)
    shape = jax.ShapeDtypeStruct(params.shape, f32)
    flat = pltpu.VMEM((rows, W), f32)
    results = pl.pallas_call(
        functools.partial(kernel, n_row, n_col),
        out_shape=(flat, flat, flat),
        in_specs=[hbm] * 5,
        out_specs=(vmem, vmem, vmem),
        scratch_shapes=[
            pltpu.VMEM((NB, ROUNDS, K), jnp.int32),
            pltpu.VMEM((ROUNDS, W), jnp.int32),
            pltpu.VMEM((ROUNDS, NB, LANES, K), bf16),
            pltpu.VMEM((ROUNDS, NB, CHUNKS * rows, K), f32),
            pltpu.VMEM((ROUNDS, NB, rows, K), f32),
            pltpu.VMEM((ROUNDS, 4, NB, rows, K), f32),
        ] + [pltpu.VMEM((NB, rows, K), f32)] * 9 + [
            pltpu.SemaphoreType.DMA((5,)),
            pltpu.SemaphoreType.DMA((ROUNDS, 4)),
            pltpu.SemaphoreType.DMA((ROUNDS, 4)),
        ],
        compiler_params=pltpu.CompilerParams(
            collective_id=0, has_side_effects=True, vmem_limit_bytes=32 * 1024 * 1024
        ),
    )(*(pltpu.with_memory_space_constraint(a, pltpu.HBM) for a in (
        params, public_copy, neighbour_mix, jnp.transpose(row_orders, (1, 0, 2)), sign_bits)))
    return pl.pallas_call(
        store_kernel,
        out_shape=(shape, shape, shape),
        in_specs=[vmem] * 3,
        out_specs=(hbm, hbm, hbm),
        scratch_shapes=[pltpu.SemaphoreType.DMA((3,))],
    )(*(pltpu.with_memory_space_constraint(a, pltpu.VMEM) for a in results))


def solution(mesh):
    split = P("row", "col", "shard", None)
    return jax.shard_map(
        functools.partial(local, mesh.shape["row"], mesh.shape["col"]),
        mesh=mesh,
        in_specs=(split, split, split, P(), P()),
        out_specs=(split, split, split),
        check_vma=False,
    )
```

```python
import functools

import jax
import jax.numpy as jnp
from jax import lax
from jax.experimental import pallas as pl
from jax.experimental.pallas import tpu as pltpu
from jax.sharding import PartitionSpec as P

W = 5120
B = 1024
K = 256
ROUNDS = 2
NB = W // B
LANES = 128
CHUNKS = B // LANES

mix_weight = 0.2
step_gamma = 0.5
decode_scale = 1.0 / K

GROUPS = ((0, 2), (2, 5))
EDGE = 8
NEXT_ROW, PREV_ROW, NEXT_COL, PREV_COL = range(4)

f32 = jnp.float32
bf16 = jnp.bfloat16


def plus_minus(value, bits):
    shift = bits
    while shift > 1:
        shift = (shift + 1) // 2
        value = value ^ (value >> shift)
    return (1 - 2 * (value & 1)).astype(f32)


def rows_of(order, count):
    return plus_minus(order & lax.broadcasted_iota(jnp.int32, (count, K), 0), 4)


def low_matrix(order):
    outer, inner = rows_of((order >> 3) & 15, 16), rows_of(order & 7, 8)
    return jnp.concatenate([outer[i:i + 1] * inner for i in range(16)], axis=0).astype(bf16)


def high_signs(order, rows):
    chunk = rows_of(order >> 7, CHUNKS)
    return jnp.concatenate([jnp.broadcast_to(chunk[i:i + 1], (rows, K)) for i in range(CHUNKS)], axis=0)


def halves(value):
    top = value.astype(bf16)
    return top, (value - top.astype(f32)).astype(bf16)


def encode(diff, low, high):
    rows = diff.shape[0]
    stacked = jnp.concatenate([diff[:, c * LANES:(c + 1) * LANES] for c in range(CHUNKS)], axis=0)
    both = jnp.concatenate(halves(stacked), axis=1)
    twice = jnp.concatenate([low, low], axis=0)
    parts = high * jnp.dot(both, twice, preferred_element_type=f32)
    return jnp.sum(parts.reshape(CHUNKS, rows, K), axis=0)


def decode(code, low, high):
    rows = code.shape[0]
    spread = high * jnp.concatenate([code] * CHUNKS, axis=0)
    both = jnp.concatenate(halves(spread), axis=0)
    result = lax.dot_general(both, low, (((1,), (1,)), ((), ())), preferred_element_type=f32)
    result = result[:CHUNKS * rows] + result[CHUNKS * rows:]
    return jnp.concatenate([result[c * rows:(c + 1) * rows] for c in range(CHUNKS)], axis=1)


def kernel(n_row, n_col, x_in, h_in, s_in, order_in, bits_in, x_v, h_v, s_v,
           order_v, bits_v, sign_v, low_v, high_v, code_v, got_v,
           self_v, base_v, rows_v, cols_v, next_v, last_v, side_v, both_v, full_v,
           in_sem, send_sem, recv_sem):
    rows = x_v.shape[0]
    row, col = lax.axis_index("row"), lax.axis_index("col")
    neighbours = (
        {"row": lax.rem(row + 1, n_row)},
        {"row": lax.rem(row + n_row - 1, n_row)},
        {"col": lax.rem(col + 1, n_col)},
        {"col": lax.rem(col + n_col - 1, n_col)},
    )

    def load(i, source, target):
        return pltpu.make_async_copy(source, target, in_sem.at[i])

    order_load = load(0, order_in.at[:, :, pl.ds(0, K)], order_v)
    bits_load = load(1, bits_in, bits_v)
    x_loads = [load(2 + j, x_in.at[0, 0, :, pl.ds(j * B, B)], x_v.at[:, pl.ds(j * B, B)]) for j in range(NB)]
    h_loads = [load(2 + NB + j, h_in.at[0, 0, :, pl.ds(j * B, B)], h_v.at[:, pl.ds(j * B, B)]) for j in range(NB)]
    s_load = load(2 + 2 * NB, s_in.at[0, 0], s_v)
    edge = lax.rem(row, EDGE) == 0
    inner = jnp.logical_not(edge)
    before_edge = lax.rem(row, EDGE) == EDGE - 1
    even = lax.rem(col, 2) == 0
    odd = jnp.logical_not(even)
    early = jnp.where(edge, PREV_ROW, NEXT_ROW)
    late = jnp.where(edge, NEXT_ROW, PREV_ROW)

    barrier = pltpu.get_barrier_semaphore()

    def greet(n):
        pl.semaphore_signal(barrier, inc=1, device_id=neighbours[n], device_id_type=pl.DeviceIdType.MESH)

    greet(NEXT_COL)
    greet(PREV_COL)
    greet(PREV_ROW)
    pl.when(jnp.logical_not(before_edge))(lambda: greet(NEXT_ROW))
    for each in [order_load, bits_load] + [load for pair in zip(x_loads, h_loads) for load in pair] + [s_load]:
        each.start()

    def build(r):
        for j in range(NB):
            order = order_v[j, r:r + 1, :]
            low_v[r, j] = low_matrix(order)
            high_v[r, j] = high_signs(order, rows)

    def columns(j):
        return slice(j * B, (j + 1) * B)

    def signs(r):
        return jnp.broadcast_to((2 * bits_v[r:r + 1, :] - 1).astype(f32), (rows, W))

    def copy(r, n, g, source):
        first, last = GROUPS[g]
        part = pl.ds(first, last - first)
        return pltpu.make_async_remote_copy(
            src_ref=source.at[part],
            dst_ref=got_v.at[r, n, part],
            send_sem=send_sem.at[r, n, g],
            recv_sem=recv_sem.at[r, n, g],
            device_id=neighbours[n],
            device_id_type=pl.DeviceIdType.MESH,
        )

    def send(r, targets, g, source):
        for n in targets:
            copy(r, n, g, source).start()

    def receive(r, sources, g):
        first, last = GROUPS[g]
        for n in sources:
            arrived = got_v.at[r, n, pl.ds(first, last - first)]
            pltpu.make_async_copy(arrived, arrived, recv_sem.at[r, n, g]).wait()

    order_load.wait()
    build(0)
    bits_load.wait()
    sign_v[0] = signs(0)
    for g, (first, last) in enumerate(GROUPS):
        for j in range(first, last):
            x_loads[j].wait()
            h_loads[j].wait()
        for j in range(first, last):
            cols = columns(j)
            code_v[0, j] = encode(sign_v[0, :, cols] * (x_v[:, cols] - h_v[:, cols]), low_v[0, j], high_v[0, j])
        if g == 0:
            pl.semaphore_wait(barrier, jnp.where(edge, 3, 4))
        send(0, (NEXT_COL, PREV_COL, NEXT_ROW), g, code_v.at[0])
        pl.when(inner)(lambda g=g: send(0, (PREV_ROW,), g, code_v.at[0]))

    build(1)
    sign_v[1] = signs(1)
    sign_v[2] = step_gamma * sign_v[0] * sign_v[1]
    s_load.wait()
    for j in range(NB):
        cols = columns(j)
        decoded = decode(decode_scale * code_v[0, j], low_v[0, j], high_v[0, j])
        update = sign_v[0, :, cols] * decoded
        public = h_v[:, cols] + update
        mixed = s_v[:, cols]
        x_v[:, cols] = x_v[:, cols] - step_gamma * public
        base = x_v[:, cols] + step_gamma * mixed - public
        h_v[:, cols] = public
        s_v[:, cols] = mixed + mix_weight * update
        self_v[j] = encode(mix_weight * sign_v[2, :, cols] * decoded, low_v[1, j], high_v[1, j])
        base_v[j] = encode(sign_v[1, :, cols] * base, low_v[1, j], high_v[1, j]) + self_v[j]

    twice = jnp.where(even, 0.0, 2.0)

    def part(j, code):
        cols = columns(j)
        decoded = decode((mix_weight * decode_scale) * code, low_v[0, j], high_v[0, j])
        s_v[:, cols] = s_v[:, cols] + sign_v[0, :, cols] * decoded
        return encode(sign_v[2, :, cols] * decoded, low_v[1, j], high_v[1, j])

    for g in range(len(GROUPS)):
        receive(0, (early,), g)
    for j in range(NB):
        rows_v[j] = part(j, got_v[0, early, j])
        next_v[j] = base_v[j] + rows_v[j]

    @pl.when(jnp.logical_and(inner, even))
    def _():
        for g in range(len(GROUPS)):
            send(1, (NEXT_ROW,), g, next_v)

    for g, (first, last) in enumerate(GROUPS):
        receive(0, (NEXT_COL, PREV_COL), g)
        for j in range(first, last):
            cols_v[j] = part(j, got_v[0, NEXT_COL, j] + got_v[0, PREV_COL, j])
            last_v[j] = base_v[j] + rows_v[j] + twice * cols_v[j]
            side_v[j] = base_v[j] + cols_v[j]
        pl.when(jnp.logical_and(inner, odd))(lambda g=g: send(1, (NEXT_ROW,), g, last_v))
        pl.when(even)(lambda g=g: send(1, (NEXT_COL, PREV_COL), g, side_v))

    for g, (first, last) in enumerate(GROUPS):
        receive(0, (late,), g)
        for j in range(first, last):
            late_part = part(j, got_v[0, late, j])
            rows_v[j] = rows_v[j] + late_part
            code_v[1, j] = last_v[j] + late_part
            both_v[j] = side_v[j] + twice * rows_v[j]
        pl.when(odd)(lambda g=g: send(1, (NEXT_COL, PREV_COL), g, both_v))
        pl.when(edge)(lambda g=g: send(1, (NEXT_ROW,), g, code_v.at[1]))
        send(1, (PREV_ROW,), g, code_v.at[1])
        pl.when(edge)(lambda g=g: send(0, (PREV_ROW,), g, code_v.at[0]))

    for j in range(NB):
        cols = columns(j)
        own = base_v[j] + rows_v[j] + cols_v[j]
        full_v[j] = own
        public = h_v[:, cols] + sign_v[1, :, cols] * decode(decode_scale * own, low_v[1, j], high_v[1, j])
        h_v[:, cols] = public
        x_v[:, cols] = x_v[:, cols] + step_gamma * (2 * s_v[:, cols] - public)

    left_out = jnp.where(lax.rem(row, EDGE) == 1, 0.0, 1.0)
    for g, (first, last) in enumerate(GROUPS):
        receive(1, range(4), g)
        for j in range(first, last):
            cols = columns(j)
            total = full_v[j] + left_out * self_v[j]
            for n in range(4):
                total = total + got_v[1, n, j]
            decoded = decode((mix_weight * decode_scale) * total, low_v[1, j], high_v[1, j])
            update = sign_v[1, :, cols] * decoded
            s_v[:, cols] = s_v[:, cols] + update
            x_v[:, cols] = x_v[:, cols] + step_gamma * update
    for r in range(ROUNDS):
        for n in range(4):
            for g in range(len(GROUPS)):
                copy(r, n, g, code_v.at[r]).wait_send()


def store_kernel(x_in, h_in, s_in, x_out, h_out, s_out, sem):
    pairs = ((x_in, x_out), (h_in, h_out), (s_in, s_out))
    copies = [pltpu.make_async_copy(a, b.at[0, 0], sem.at[i]) for i, (a, b) in enumerate(pairs)]
    for copy in copies:
        copy.start()
    for copy in copies:
        copy.wait()


def local(n_row, n_col, params, public_copy, neighbour_mix, row_orders, sign_bits):
    rows = params.shape[2]
    hbm = pl.BlockSpec(memory_space=pltpu.HBM)
    vmem = pl.BlockSpec(memory_space=pltpu.VMEM)
    shape = jax.ShapeDtypeStruct(params.shape, f32)
    flat = pltpu.VMEM((rows, W), f32)
    results = pl.pallas_call(
        functools.partial(kernel, n_row, n_col),
        out_shape=(flat, flat, flat),
        in_specs=[hbm] * 5,
        out_specs=(vmem, vmem, vmem),
        scratch_shapes=[
            pltpu.VMEM((NB, ROUNDS, K), jnp.int32),
            pltpu.VMEM((ROUNDS, W), jnp.int32),
            pltpu.VMEM((3, rows, W), f32),
            pltpu.VMEM((ROUNDS, NB, LANES, K), bf16),
            pltpu.VMEM((ROUNDS, NB, CHUNKS * rows, K), f32),
            pltpu.VMEM((ROUNDS, NB, rows, K), f32),
            pltpu.VMEM((ROUNDS, 4, NB, rows, K), f32),
        ] + [pltpu.VMEM((NB, rows, K), f32)] * 9 + [
            pltpu.SemaphoreType.DMA((3 + 2 * NB,)),
            pltpu.SemaphoreType.DMA((ROUNDS, 4, len(GROUPS))),
            pltpu.SemaphoreType.DMA((ROUNDS, 4, len(GROUPS))),
        ],
        compiler_params=pltpu.CompilerParams(
            collective_id=0, has_side_effects=True, vmem_limit_bytes=32 * 1024 * 1024
        ),
    )(*(pltpu.with_memory_space_constraint(a, pltpu.HBM) for a in (
        params, public_copy, neighbour_mix, jnp.transpose(row_orders, (1, 0, 2)), sign_bits)))
    return pl.pallas_call(
        store_kernel,
        out_shape=(shape, shape, shape),
        in_specs=[vmem] * 3,
        out_specs=(hbm, hbm, hbm),
        scratch_shapes=[pltpu.SemaphoreType.DMA((3,))],
    )(*(pltpu.with_memory_space_constraint(a, pltpu.VMEM) for a in results))


def solution(mesh):
    split = P("row", "col", "shard", None)
    return jax.shard_map(
        functools.partial(local, mesh.shape["row"], mesh.shape["col"]),
        mesh=mesh,
        in_specs=(split, split, split, P(), P()),
        out_specs=(split, split, split),
        check_vma=False,
    )
```

```python
import functools

import jax
import jax.numpy as jnp
from jax import lax
from jax.experimental import pallas as pl
from jax.experimental.pallas import tpu as pltpu
from jax.sharding import PartitionSpec as P

W = 5120
B = 1024
K = 256
ROUNDS = 2
NB = W // B
LANES = 128
CHUNKS = B // LANES

mix_weight = 0.2
step_gamma = 0.5
decode_scale = 1.0 / K

GROUPS = ((0, 2), (2, 5))
EDGE = 8
NEXT_ROW, PREV_ROW, CHIP, SIDE = range(4)

f32 = jnp.float32
bf16 = jnp.bfloat16


def plus_minus(value, bits):
    shift = bits
    while shift > 1:
        shift = (shift + 1) // 2
        value = value ^ (value >> shift)
    return (1 - 2 * (value & 1)).astype(f32)


def rows_of(order, count):
    return plus_minus(order & lax.broadcasted_iota(jnp.int32, (count, K), 0), 4)


def low_matrix(order):
    outer, inner = rows_of((order >> 3) & 15, 16), rows_of(order & 7, 8)
    return jnp.concatenate([outer[i:i + 1] * inner for i in range(16)], axis=0).astype(bf16)


def high_signs(order, rows):
    chunk = rows_of(order >> 7, CHUNKS)
    return jnp.concatenate([jnp.broadcast_to(chunk[i:i + 1], (rows, K)) for i in range(CHUNKS)], axis=0)


def halves(value):
    top = value.astype(bf16)
    return top, (value - top.astype(f32)).astype(bf16)


def encode(diff, low, high):
    rows = diff.shape[0]
    stacked = jnp.concatenate([diff[:, c * LANES:(c + 1) * LANES] for c in range(CHUNKS)], axis=0)
    both = jnp.concatenate(halves(stacked), axis=1)
    twice = jnp.concatenate([low, low], axis=0)
    parts = high * jnp.dot(both, twice, preferred_element_type=f32)
    return jnp.sum(parts.reshape(CHUNKS, rows, K), axis=0)


def decode(code, low, high):
    rows = code.shape[0]
    spread = high * jnp.concatenate([code] * CHUNKS, axis=0)
    both = jnp.concatenate(halves(spread), axis=0)
    result = lax.dot_general(both, low, (((1,), (1,)), ((), ())), preferred_element_type=f32)
    result = result[:CHUNKS * rows] + result[CHUNKS * rows:]
    return jnp.concatenate([result[c * rows:(c + 1) * rows] for c in range(CHUNKS)], axis=1)


def kernel(n_row, n_col, x_in, h_in, s_in, order_in, bits_in, x_v, h_v, s_v,
           order_v, bits_v, sign_v, low_v, high_v, code_v, got_v,
           self_v, base_v, rows_v, cols_v, next_v, last_v, side_v, both_v, full_v,
           more_v, out_v, aside_v, back_v,
           in_sem, send_sem, recv_sem, aside_sem, ready):
    rows = x_v.shape[0]
    row, col = lax.axis_index("row"), lax.axis_index("col")
    even = lax.rem(col, 2) == 0
    odd = jnp.logical_not(even)
    chip_col = jnp.where(even, col + 1, col - 1)
    side_col = lax.rem(jnp.where(even, col + n_col - 1, col + 1), n_col)
    next_row, prev_row = lax.rem(row + 1, n_row), lax.rem(row + n_row - 1, n_row)
    neighbours = ({"row": next_row}, {"row": prev_row}, {"col": chip_col}, {"col": side_col})

    def load(i, source, target):
        return pltpu.make_async_copy(source, target, in_sem.at[i])

    order_load = load(0, order_in.at[:, :, pl.ds(0, K)], order_v)
    bits_load = load(1, bits_in, bits_v)
    x_loads = [load(2 + j, x_in.at[0, 0, :, pl.ds(j * B, B)], x_v.at[:, pl.ds(j * B, B)]) for j in range(NB)]
    h_loads = [load(2 + NB + j, h_in.at[0, 0, :, pl.ds(j * B, B)], h_v.at[:, pl.ds(j * B, B)]) for j in range(NB)]
    s_load = load(2 + 2 * NB, s_in.at[0, 0], s_v)
    edge = lax.rem(row, EDGE) == 0
    inner = jnp.logical_not(edge)
    before_edge = lax.rem(row, EDGE) == EDGE - 1
    early = jnp.where(edge, PREV_ROW, NEXT_ROW)
    late = jnp.where(edge, NEXT_ROW, PREV_ROW)
    pair = jnp.where(even, side_col, col) // 2
    middle = n_col // 4
    lopsided = jnp.logical_or(pair < middle, pair == n_col // 2 - 1)
    first_side = jnp.logical_and(lopsided, (pair < middle) == odd)
    last_side = jnp.logical_not(first_side)
    at_cut = jnp.logical_or(pair < middle, pair == n_col // 2 - 1)
    two_before = lax.rem(row, EDGE) == EDGE - 2
    aside_from = jnp.logical_and(even, jnp.logical_or(two_before, jnp.logical_and(before_edge, at_cut)))
    aside_by = jnp.logical_and(before_edge, jnp.logical_and(odd, at_cut))
    aside_to = jnp.logical_and(edge, jnp.logical_or(even, at_cut))
    at_end = pair == n_col // 2 - 1
    back_from = jnp.logical_and(before_edge, jnp.logical_and(odd, at_end))
    back_by = jnp.logical_and(edge, jnp.logical_and(odd, at_end))
    back_to = jnp.logical_and(edge, jnp.logical_and(even, at_end))
    aside_target = {
        "row": jnp.where(before_edge, next_row, lax.rem(row + 2, n_row)),
        "col": jnp.where(before_edge, side_col, col),
    }
    aside_source = {
        "row": jnp.where(odd, prev_row, lax.rem(row + n_row - 2, n_row)),
        "col": jnp.where(odd, side_col, col),
    }

    barrier = pltpu.get_barrier_semaphore()

    def greet(device):
        pl.semaphore_signal(barrier, inc=1, device_id=device, device_id_type=pl.DeviceIdType.MESH)

    pl.when(jnp.logical_or(first_side, jnp.logical_not(lopsided)))(lambda: greet(neighbours[SIDE]))
    greet(neighbours[CHIP])
    greet(neighbours[PREV_ROW])
    pl.when(jnp.logical_not(before_edge))(lambda: greet(neighbours[NEXT_ROW]))
    pl.when(aside_to)(lambda: greet(aside_source))
    pl.when(back_to)(lambda: greet({"row": prev_row, "col": side_col}))
    greetings = 1 + jnp.where(edge, 1, 2) + jnp.where(first_side, 0, 1) + jnp.where(jnp.logical_or(aside_from, back_from), 1, 0)

    for each in [order_load, bits_load] + [load for pair in zip(x_loads, h_loads) for load in pair] + [s_load]:
        each.start()

    def build(r):
        for j in range(NB):
            order = order_v[j, r:r + 1, :]
            low_v[r, j] = low_matrix(order)
            high_v[r, j] = high_signs(order, rows)

    def columns(j):
        return slice(j * B, (j + 1) * B)

    def signs(r):
        return jnp.broadcast_to((2 * bits_v[r:r + 1, :] - 1).astype(f32), (rows, W))

    def copy(r, n, g, source):
        first, last = GROUPS[g]
        part = pl.ds(first, last - first)
        return pltpu.make_async_remote_copy(
            src_ref=source.at[part],
            dst_ref=got_v.at[r, n, part],
            send_sem=send_sem.at[r, n, g],
            recv_sem=recv_sem.at[r, n, g],
            device_id=neighbours[n],
            device_id_type=pl.DeviceIdType.MESH,
        )

    def send(r, targets, g, source):
        for n in targets:
            copy(r, n, g, source).start()

    def copy_aside(g):
        first, last = GROUPS[g]
        part = pl.ds(first, last - first)
        return pltpu.make_async_remote_copy(
            src_ref=code_v.at[0, part],
            dst_ref=aside_v.at[part],
            send_sem=aside_sem.at[0, g],
            recv_sem=aside_sem.at[1, g],
            device_id=aside_target,
            device_id_type=pl.DeviceIdType.MESH,
        )

    def copy_back(g):
        first, last = GROUPS[g]
        part = pl.ds(first, last - first)
        return pltpu.make_async_remote_copy(
            src_ref=code_v.at[0, part],
            dst_ref=back_v.at[part],
            send_sem=aside_sem.at[2, g],
            recv_sem=aside_sem.at[3, g],
            device_id={"row": next_row, "col": side_col},
            device_id_type=pl.DeviceIdType.MESH,
        )

    def receive(r, sources, g):
        first, last = GROUPS[g]
        for n in sources:
            arrived = got_v.at[r, n, pl.ds(first, last - first)]
            pltpu.make_async_copy(arrived, arrived, recv_sem.at[r, n, g]).wait()

    signals = jnp.logical_and(lopsided, last_side)

    @pl.when(signals)
    def _():
        pl.semaphore_wait(barrier, greetings)
        pl.semaphore_signal(ready, inc=1, device_id=neighbours[SIDE], device_id_type=pl.DeviceIdType.MESH)

    order_load.wait()
    build(0)
    bits_load.wait()
    sign_v[0] = signs(0)
    for g, (first, last) in enumerate(GROUPS):
        for j in range(first, last):
            x_loads[j].wait()
            h_loads[j].wait()
        for j in range(first, last):
            cols = columns(j)
            code_v[0, j] = encode(sign_v[0, :, cols] * (x_v[:, cols] - h_v[:, cols]), low_v[0, j], high_v[0, j])
        if g == 0:
            pl.when(jnp.logical_not(signals))(lambda: pl.semaphore_wait(barrier, greetings))
        pl.when(last_side)(lambda g=g: send(0, (SIDE,), g, code_v.at[0]))
        pl.when(aside_from)(lambda g=g: copy_aside(g).start())
        pl.when(back_from)(lambda g=g: copy_back(g).start())
        send(0, (CHIP, NEXT_ROW), g, code_v.at[0])
        pl.when(inner)(lambda g=g: send(0, (PREV_ROW,), g, code_v.at[0]))

    build(1)
    sign_v[1] = signs(1)
    sign_v[2] = step_gamma * sign_v[0] * sign_v[1]
    left_out = jnp.where(lax.rem(row, EDGE) == 1, 0.0, 1.0)
    s_load.wait()
    for j in range(NB):
        cols = columns(j)
        decoded = decode(decode_scale * code_v[0, j], low_v[0, j], high_v[0, j])
        update = sign_v[0, :, cols] * decoded
        public = h_v[:, cols] + update
        mixed = s_v[:, cols]
        x_v[:, cols] = x_v[:, cols] - step_gamma * public
        base = x_v[:, cols] + step_gamma * mixed - public
        h_v[:, cols] = public
        s_v[:, cols] = mixed + mix_weight * update
        self_v[j] = encode(mix_weight * sign_v[2, :, cols] * decoded, low_v[1, j], high_v[1, j])
        more_v[j] = left_out * self_v[j]
        base_v[j] = encode(sign_v[1, :, cols] * base, low_v[1, j], high_v[1, j]) + self_v[j]

    twice = jnp.where(even, 0.0, 2.0)

    def part(j, code, mix=True):
        cols = columns(j)
        decoded = decode((mix_weight * decode_scale) * code, low_v[0, j], high_v[0, j])
        if mix:
            s_v[:, cols] = s_v[:, cols] + sign_v[0, :, cols] * decoded
        return encode(sign_v[2, :, cols] * decoded, low_v[1, j], high_v[1, j])

    @pl.when(jnp.logical_and(before_edge, even))
    def _():
        for g in range(len(GROUPS)):
            send(1, (NEXT_ROW,), g, base_v)

    for g in range(len(GROUPS)):
        receive(0, (CHIP,), g)
    for j in range(NB):
        cols_v[j] = part(j, got_v[0, CHIP, j])

    @pl.when(first_side)
    def _():
        pl.semaphore_wait(ready, 1)
        for g in range(len(GROUPS)):
            send(0, (SIDE,), g, code_v.at[0])

    for g in range(len(GROUPS)):
        receive(0, (early,), g)
    for j in range(NB):
        rows_v[j] = part(j, got_v[0, early, j])
        next_v[j] = base_v[j] + rows_v[j] + twice * cols_v[j]

    @pl.when(jnp.logical_or(jnp.logical_and(jnp.logical_and(inner, even), jnp.logical_not(before_edge)), aside_by))
    def _():
        for g in range(len(GROUPS)):
            send(1, (NEXT_ROW,), g, next_v)

    for g, (first, last) in enumerate(GROUPS):
        receive(0, (SIDE,), g)
        for j in range(first, last):
            side_part = part(j, got_v[0, SIDE, j])
            last_v[j] = next_v[j] + twice * side_part
            cols_v[j] = cols_v[j] + side_part
            side_v[j] = base_v[j] + cols_v[j]
            both_v[j] = side_v[j] + twice * rows_v[j]
        pl.when(jnp.logical_and(jnp.logical_and(inner, odd), jnp.logical_not(aside_by)))(
            lambda g=g: send(1, (NEXT_ROW,), g, last_v)
        )
        pl.when(even)(lambda g=g: send(1, (CHIP, SIDE), g, side_v))
        pl.when(back_by)(lambda g=g: send(1, (SIDE,), g, both_v))

    for g, (first, last) in enumerate(GROUPS):
        receive(0, (late,), g)
        for j in range(first, last):
            late_part = part(j, got_v[0, late, j])
            rows_v[j] = rows_v[j] + late_part
            code_v[1, j] = last_v[j] + late_part
            out_v[j] = side_v[j] + twice * rows_v[j]
        pl.when(jnp.logical_and(odd, jnp.logical_not(back_by)))(lambda g=g: send(1, (SIDE,), g, out_v))
        pl.when(odd)(lambda g=g: send(1, (CHIP,), g, out_v))
        pl.when(edge)(lambda g=g: send(1, (NEXT_ROW,), g, code_v.at[1]))
        send(1, (PREV_ROW,), g, code_v.at[1])
        pl.when(edge)(lambda g=g: send(0, (PREV_ROW,), g, code_v.at[0]))

    for j in range(NB):
        cols = columns(j)
        own = base_v[j] + rows_v[j] + cols_v[j]
        full_v[j] = own
        public = h_v[:, cols] + sign_v[1, :, cols] * decode(decode_scale * own, low_v[1, j], high_v[1, j])
        h_v[:, cols] = public
        x_v[:, cols] = x_v[:, cols] + step_gamma * (2 * s_v[:, cols] - public)

    @pl.when(aside_to)
    def _():
        for g in range(len(GROUPS)):
            copy_aside(g).wait_recv()
        for j in range(NB):
            more_v[j] = more_v[j] + jnp.where(odd, 2.0, 1.0) * part(j, aside_v[j], mix=False)

    @pl.when(back_to)
    def _():
        for g in range(len(GROUPS)):
            copy_back(g).wait_recv()
        for j in range(NB):
            more_v[j] = more_v[j] + 2 * part(j, back_v[j], mix=False)

    for g, (first, last) in enumerate(GROUPS):
        receive(1, range(4), g)
        for j in range(first, last):
            cols = columns(j)
            total = full_v[j] + more_v[j]
            for n in range(4):
                total = total + got_v[1, n, j]
            decoded = decode((mix_weight * decode_scale) * total, low_v[1, j], high_v[1, j])
            update = sign_v[1, :, cols] * decoded
            s_v[:, cols] = s_v[:, cols] + update
            x_v[:, cols] = x_v[:, cols] + step_gamma * update
    for r in range(ROUNDS):
        for n in range(4):
            for g in range(len(GROUPS)):
                copy(r, n, g, code_v.at[r]).wait_send()

    @pl.when(aside_from)
    def _():
        for g in range(len(GROUPS)):
            copy_aside(g).wait_send()

    @pl.when(back_from)
    def _():
        for g in range(len(GROUPS)):
            copy_back(g).wait_send()


def store_kernel(x_in, h_in, s_in, x_out, h_out, s_out, sem):
    pairs = ((x_in, x_out), (h_in, h_out), (s_in, s_out))
    copies = [pltpu.make_async_copy(a, b.at[0, 0], sem.at[i]) for i, (a, b) in enumerate(pairs)]
    for copy in copies:
        copy.start()
    for copy in copies:
        copy.wait()


def local(n_row, n_col, params, public_copy, neighbour_mix, row_orders, sign_bits):
    rows = params.shape[2]
    hbm = pl.BlockSpec(memory_space=pltpu.HBM)
    vmem = pl.BlockSpec(memory_space=pltpu.VMEM)
    shape = jax.ShapeDtypeStruct(params.shape, f32)
    flat = pltpu.VMEM((rows, W), f32)
    results = pl.pallas_call(
        functools.partial(kernel, n_row, n_col),
        out_shape=(flat, flat, flat),
        in_specs=[hbm] * 5,
        out_specs=(vmem, vmem, vmem),
        scratch_shapes=[
            pltpu.VMEM((NB, ROUNDS, K), jnp.int32),
            pltpu.VMEM((ROUNDS, W), jnp.int32),
            pltpu.VMEM((3, rows, W), f32),
            pltpu.VMEM((ROUNDS, NB, LANES, K), bf16),
            pltpu.VMEM((ROUNDS, NB, CHUNKS * rows, K), f32),
            pltpu.VMEM((ROUNDS, NB, rows, K), f32),
            pltpu.VMEM((ROUNDS, 4, NB, rows, K), f32),
        ] + [pltpu.VMEM((NB, rows, K), f32)] * 13 + [
            pltpu.SemaphoreType.DMA((3 + 2 * NB,)),
            pltpu.SemaphoreType.DMA((ROUNDS, 4, len(GROUPS))),
            pltpu.SemaphoreType.DMA((ROUNDS, 4, len(GROUPS))),
            pltpu.SemaphoreType.DMA((4, len(GROUPS))),
            pltpu.SemaphoreType.REGULAR,
        ],
        compiler_params=pltpu.CompilerParams(
            collective_id=0, has_side_effects=True, vmem_limit_bytes=32 * 1024 * 1024
        ),
    )(*(pltpu.with_memory_space_constraint(a, pltpu.HBM) for a in (
        params, public_copy, neighbour_mix, jnp.transpose(row_orders, (1, 0, 2)), sign_bits)))
    return pl.pallas_call(
        store_kernel,
        out_shape=(shape, shape, shape),
        in_specs=[vmem] * 3,
        out_specs=(hbm, hbm, hbm),
        scratch_shapes=[pltpu.SemaphoreType.DMA((3,))],
    )(*(pltpu.with_memory_space_constraint(a, pltpu.VMEM) for a in results))


def solution(mesh):
    split = P("row", "col", "shard", None)
    return jax.shard_map(
        functools.partial(local, mesh.shape["row"], mesh.shape["col"]),
        mesh=mesh,
        in_specs=(split, split, split, P(), P()),
        out_specs=(split, split, split),
        check_vma=False,
    )
```

```python
import functools

import jax
import jax.numpy as jnp
from jax import lax
from jax.experimental import pallas as pl
from jax.experimental.pallas import tpu as pltpu
from jax.sharding import PartitionSpec as P

W = 5120
B = 1024
K = 256
ROUNDS = 2
NB = W // B
LANES = 128
CHUNKS = B // LANES

mix_weight = 0.2
step_gamma = 0.5
decode_scale = 1.0 / K

GROUPS = ((0, 2), (2, 5))
EDGE = 8
NEXT_ROW, PREV_ROW, CHIP, SIDE = range(4)

f32 = jnp.float32
bf16 = jnp.bfloat16


def plus_minus(value, bits):
    shift = bits
    while shift > 1:
        shift = (shift + 1) // 2
        value = value ^ (value >> shift)
    return (1 - 2 * (value & 1)).astype(f32)


def rows_of(order, count):
    return plus_minus(order & lax.broadcasted_iota(jnp.int32, (count, K), 0), 4)


def low_matrix(order):
    outer, inner = rows_of((order >> 3) & 15, 16), rows_of(order & 7, 8)
    return jnp.concatenate([outer[i:i + 1] * inner for i in range(16)], axis=0).astype(bf16)


def high_signs(order, rows):
    chunk = rows_of(order >> 7, CHUNKS)
    return jnp.concatenate([jnp.broadcast_to(chunk[i:i + 1], (rows, K)) for i in range(CHUNKS)], axis=0)


def halves(value):
    top = value.astype(bf16)
    return top, (value - top.astype(f32)).astype(bf16)


def encode(diff, low, high):
    rows = diff.shape[0]
    stacked = jnp.concatenate([diff[:, c * LANES:(c + 1) * LANES] for c in range(CHUNKS)], axis=0)
    both = jnp.concatenate(halves(stacked), axis=1)
    twice = jnp.concatenate([low, low], axis=0)
    parts = high * jnp.dot(both, twice, preferred_element_type=f32)
    return jnp.sum(parts.reshape(CHUNKS, rows, K), axis=0)


def decode(code, low, high):
    rows = code.shape[0]
    spread = high * jnp.concatenate([code] * CHUNKS, axis=0)
    both = jnp.concatenate(halves(spread), axis=0)
    result = lax.dot_general(both, low, (((1,), (1,)), ((), ())), preferred_element_type=f32)
    result = result[:CHUNKS * rows] + result[CHUNKS * rows:]
    return jnp.concatenate([result[c * rows:(c + 1) * rows] for c in range(CHUNKS)], axis=1)


def kernel(n_row, n_col, x_in, h_in, s_in, order_in, bits_in, x_v, h_v, s_v, total_v, low1_v, high1_v, sign1_v,
           order_v, bits_v, sign0_v, low0_v, high0_v, code_v, got_v,
           self_v, base_v, rows_v, cols_v, next_v, last_v, side_v, both_v, full_v,
           more_v, out_v, aside_v, back_v,
           in_sem, send_sem, recv_sem, aside_sem, ready):
    rows = x_v.shape[0]
    row, col = lax.axis_index("row"), lax.axis_index("col")
    even = lax.rem(col, 2) == 0
    odd = jnp.logical_not(even)
    chip_col = jnp.where(even, col + 1, col - 1)
    side_col = lax.rem(jnp.where(even, col + n_col - 1, col + 1), n_col)
    next_row, prev_row = lax.rem(row + 1, n_row), lax.rem(row + n_row - 1, n_row)
    neighbours = ({"row": next_row}, {"row": prev_row}, {"col": chip_col}, {"col": side_col})

    def load(i, source, target):
        return pltpu.make_async_copy(source, target, in_sem.at[i])

    order_load = load(0, order_in.at[:, :, pl.ds(0, K)], order_v)
    bits_load = load(1, bits_in, bits_v)
    x_loads = [load(2 + j, x_in.at[0, 0, :, pl.ds(j * B, B)], x_v.at[:, pl.ds(j * B, B)]) for j in range(NB)]
    h_loads = [load(2 + NB + j, h_in.at[0, 0, :, pl.ds(j * B, B)], h_v.at[:, pl.ds(j * B, B)]) for j in range(NB)]
    s_load = load(2 + 2 * NB, s_in.at[0, 0], s_v)
    edge = lax.rem(row, EDGE) == 0
    inner = jnp.logical_not(edge)
    before_edge = lax.rem(row, EDGE) == EDGE - 1
    early = jnp.where(edge, PREV_ROW, NEXT_ROW)
    late = jnp.where(edge, NEXT_ROW, PREV_ROW)
    pair = jnp.where(even, side_col, col) // 2
    middle = n_col // 4
    lopsided = jnp.logical_or(pair < middle, pair == n_col // 2 - 1)
    first_side = jnp.logical_and(lopsided, (pair < middle) == odd)
    last_side = jnp.logical_not(first_side)
    at_cut = jnp.logical_or(pair < middle, pair == n_col // 2 - 1)
    two_before = lax.rem(row, EDGE) == EDGE - 2
    aside_from = jnp.logical_and(even, jnp.logical_or(two_before, jnp.logical_and(before_edge, at_cut)))
    aside_by = jnp.logical_and(before_edge, jnp.logical_and(odd, at_cut))
    aside_to = jnp.logical_and(edge, jnp.logical_or(even, at_cut))
    at_end = pair == n_col // 2 - 1
    back_from = jnp.logical_and(before_edge, jnp.logical_and(odd, at_end))
    back_by = jnp.logical_and(edge, jnp.logical_and(odd, at_end))
    back_to = jnp.logical_and(edge, jnp.logical_and(even, at_end))
    aside_target = {
        "row": jnp.where(before_edge, next_row, lax.rem(row + 2, n_row)),
        "col": jnp.where(before_edge, side_col, col),
    }
    aside_source = {
        "row": jnp.where(odd, prev_row, lax.rem(row + n_row - 2, n_row)),
        "col": jnp.where(odd, side_col, col),
    }

    barrier = pltpu.get_barrier_semaphore()

    def greet(device):
        pl.semaphore_signal(barrier, inc=1, device_id=device, device_id_type=pl.DeviceIdType.MESH)

    pl.when(jnp.logical_or(first_side, jnp.logical_not(lopsided)))(lambda: greet(neighbours[SIDE]))
    greet(neighbours[CHIP])
    greet(neighbours[PREV_ROW])
    pl.when(jnp.logical_not(before_edge))(lambda: greet(neighbours[NEXT_ROW]))
    pl.when(aside_to)(lambda: greet(aside_source))
    pl.when(back_to)(lambda: greet({"row": prev_row, "col": side_col}))
    greetings = 1 + jnp.where(edge, 1, 2) + jnp.where(first_side, 0, 1) + jnp.where(jnp.logical_or(aside_from, back_from), 1, 0)

    for each in [order_load, bits_load] + [load for pair in zip(x_loads, h_loads) for load in pair] + [s_load]:
        each.start()

    low_v, high_v = (low0_v, low1_v), (high0_v, high1_v)

    def build(r):
        for j in range(NB):
            order = order_v[j, r:r + 1, :]
            low_v[r][j] = low_matrix(order)
            high_v[r][j] = high_signs(order, rows)

    def columns(j):
        return slice(j * B, (j + 1) * B)

    def signs(r):
        return jnp.broadcast_to((2 * bits_v[r:r + 1, :] - 1).astype(f32), (rows, W))

    def copy(r, n, g, source):
        first, last = GROUPS[g]
        part = pl.ds(first, last - first)
        return pltpu.make_async_remote_copy(
            src_ref=source.at[part],
            dst_ref=got_v.at[r, n, part],
            send_sem=send_sem.at[r, n, g],
            recv_sem=recv_sem.at[r, n, g],
            device_id=neighbours[n],
            device_id_type=pl.DeviceIdType.MESH,
        )

    def send(r, targets, g, source):
        for n in targets:
            copy(r, n, g, source).start()

    def copy_aside(g):
        first, last = GROUPS[g]
        part = pl.ds(first, last - first)
        return pltpu.make_async_remote_copy(
            src_ref=code_v.at[0, part],
            dst_ref=aside_v.at[part],
            send_sem=aside_sem.at[0, g],
            recv_sem=aside_sem.at[1, g],
            device_id=aside_target,
            device_id_type=pl.DeviceIdType.MESH,
        )

    def copy_back(g):
        first, last = GROUPS[g]
        part = pl.ds(first, last - first)
        return pltpu.make_async_remote_copy(
            src_ref=code_v.at[0, part],
            dst_ref=back_v.at[part],
            send_sem=aside_sem.at[2, g],
            recv_sem=aside_sem.at[3, g],
            device_id={"row": next_row, "col": side_col},
            device_id_type=pl.DeviceIdType.MESH,
        )

    def receive(r, sources, g):
        first, last = GROUPS[g]
        for n in sources:
            arrived = got_v.at[r, n, pl.ds(first, last - first)]
            pltpu.make_async_copy(arrived, arrived, recv_sem.at[r, n, g]).wait()

    signals = jnp.logical_and(lopsided, last_side)

    @pl.when(signals)
    def _():
        pl.semaphore_wait(barrier, greetings)
        pl.semaphore_signal(ready, inc=1, device_id=neighbours[SIDE], device_id_type=pl.DeviceIdType.MESH)

    order_load.wait()
    build(0)
    bits_load.wait()
    sign0_v[0] = signs(0)
    for g, (first, last) in enumerate(GROUPS):
        for j in range(first, last):
            x_loads[j].wait()
            h_loads[j].wait()
        for j in range(first, last):
            cols = columns(j)
            code_v[0, j] = encode(sign0_v[0, :, cols] * (x_v[:, cols] - h_v[:, cols]), low0_v[j], high0_v[j])
        if g == 0:
            pl.when(jnp.logical_not(signals))(lambda: pl.semaphore_wait(barrier, greetings))
        pl.when(aside_from)(lambda g=g: copy_aside(g).start())
        pl.when(last_side)(lambda g=g: send(0, (SIDE,), g, code_v.at[0]))
        pl.when(back_from)(lambda g=g: copy_back(g).start())
        send(0, (CHIP, NEXT_ROW), g, code_v.at[0])
        pl.when(inner)(lambda g=g: send(0, (PREV_ROW,), g, code_v.at[0]))

    build(1)
    sign1_v[...] = signs(1)
    sign0_v[1] = step_gamma * sign0_v[0] * sign1_v[...]
    left_out = jnp.where(lax.rem(row, EDGE) == 1, 0.0, 1.0)
    s_load.wait()
    for j in range(NB):
        cols = columns(j)
        decoded = decode(decode_scale * code_v[0, j], low0_v[j], high0_v[j])
        update = sign0_v[0, :, cols] * decoded
        public = h_v[:, cols] + update
        mixed = s_v[:, cols]
        x_v[:, cols] = x_v[:, cols] - step_gamma * public
        base = x_v[:, cols] + step_gamma * mixed - public
        h_v[:, cols] = public
        s_v[:, cols] = mixed + mix_weight * update
        self_v[j] = encode(mix_weight * sign0_v[1, :, cols] * decoded, low1_v[j], high1_v[j])
        more_v[j] = left_out * self_v[j]
        base_v[j] = encode(sign1_v[:, cols] * base, low1_v[j], high1_v[j]) + self_v[j]

    twice = jnp.where(even, 0.0, 2.0)

    def part(j, code, mix=True):
        cols = columns(j)
        decoded = decode((mix_weight * decode_scale) * code, low0_v[j], high0_v[j])
        if mix:
            s_v[:, cols] = s_v[:, cols] + sign0_v[0, :, cols] * decoded
        return encode(sign0_v[1, :, cols] * decoded, low1_v[j], high1_v[j])

    @pl.when(jnp.logical_and(before_edge, even))
    def _():
        for g in range(len(GROUPS)):
            send(1, (NEXT_ROW,), g, base_v)

    for g in range(len(GROUPS)):
        receive(0, (CHIP,), g)
    for j in range(NB):
        cols_v[j] = part(j, got_v[0, CHIP, j])

    @pl.when(first_side)
    def _():
        pl.semaphore_wait(ready, 1)
        for g in range(len(GROUPS)):
            send(0, (SIDE,), g, code_v.at[0])

    for g in range(len(GROUPS)):
        receive(0, (early,), g)
    for j in range(NB):
        rows_v[j] = part(j, got_v[0, early, j])
        next_v[j] = base_v[j] + rows_v[j] + twice * cols_v[j]

    @pl.when(jnp.logical_or(jnp.logical_and(jnp.logical_and(inner, even), jnp.logical_not(before_edge)), aside_by))
    def _():
        for g in range(len(GROUPS)):
            send(1, (NEXT_ROW,), g, next_v)

    for g, (first, last) in enumerate(GROUPS):
        receive(0, (SIDE,), g)
        for j in range(first, last):
            side_part = part(j, got_v[0, SIDE, j])
            last_v[j] = next_v[j] + twice * side_part
            cols_v[j] = cols_v[j] + side_part
            side_v[j] = base_v[j] + cols_v[j]
            both_v[j] = side_v[j] + twice * rows_v[j]
        pl.when(jnp.logical_and(jnp.logical_and(inner, odd), jnp.logical_not(aside_by)))(
            lambda g=g: send(1, (NEXT_ROW,), g, last_v)
        )
        pl.when(even)(lambda g=g: send(1, (CHIP, SIDE), g, side_v))
        pl.when(back_by)(lambda g=g: send(1, (SIDE,), g, both_v))

    for g, (first, last) in enumerate(GROUPS):
        receive(0, (late,), g)
        for j in range(first, last):
            late_part = part(j, got_v[0, late, j])
            rows_v[j] = rows_v[j] + late_part
            code_v[1, j] = last_v[j] + late_part
            out_v[j] = side_v[j] + twice * rows_v[j]
        pl.when(jnp.logical_and(odd, jnp.logical_not(back_by)))(lambda g=g: send(1, (SIDE,), g, out_v))
        pl.when(odd)(lambda g=g: send(1, (CHIP,), g, out_v))
        pl.when(edge)(lambda g=g: send(1, (NEXT_ROW,), g, code_v.at[1]))
        send(1, (PREV_ROW,), g, code_v.at[1])
        pl.when(edge)(lambda g=g: send(0, (PREV_ROW,), g, code_v.at[0]))

    for j in range(NB):
        cols = columns(j)
        own = base_v[j] + rows_v[j] + cols_v[j]
        full_v[j] = own
        public = h_v[:, cols] + sign1_v[:, cols] * decode(decode_scale * own, low1_v[j], high1_v[j])
        h_v[:, cols] = public
        x_v[:, cols] = x_v[:, cols] + step_gamma * (2 * s_v[:, cols] - public)

    @pl.when(aside_to)
    def _():
        for g, (first, last) in enumerate(GROUPS):
            copy_aside(g).wait_recv()
            for j in range(first, last):
                more_v[j] = more_v[j] + jnp.where(odd, 2.0, 1.0) * part(j, aside_v[j], mix=False)

    @pl.when(back_to)
    def _():
        for g in range(len(GROUPS)):
            copy_back(g).wait_recv()
        for j in range(NB):
            more_v[j] = more_v[j] + 2 * part(j, back_v[j], mix=False)

    for g, (first, last) in enumerate(GROUPS):
        receive(1, range(4), g)
        for j in range(first, last):
            total = full_v[j] + more_v[j]
            for n in range(4):
                total = total + got_v[1, n, j]
            total_v[j] = (mix_weight * decode_scale) * total
    for r in range(ROUNDS):
        for n in range(4):
            for g in range(len(GROUPS)):
                copy(r, n, g, code_v.at[r]).wait_send()

    @pl.when(aside_from)
    def _():
        for g in range(len(GROUPS)):
            copy_aside(g).wait_send()

    @pl.when(back_from)
    def _():
        for g in range(len(GROUPS)):
            copy_back(g).wait_send()


def last_kernel(x_in, h_in, s_in, total, low, high, sign, x_out, h_out, s_out, x_v, s_v, sem):
    copies = [pltpu.make_async_copy(h_in, h_out.at[0, 0], sem.at[0])]
    copies[0].start()
    for j in range(NB):
        cols = pl.ds(j * B, B)
        update = sign[:, cols] * decode(total[j], low[j], high[j])
        s_v[:, cols] = s_in[:, cols] + update
        x_v[:, cols] = x_in[:, cols] + step_gamma * update
        for i, (source, target) in enumerate(((s_v, s_out), (x_v, x_out))):
            copies.append(pltpu.make_async_copy(source.at[:, cols], target.at[0, 0, :, cols], sem.at[1 + 2 * j + i]))
            copies[-1].start()
    for copy in copies:
        copy.wait()


def local(n_row, n_col, params, public_copy, neighbour_mix, row_orders, sign_bits):
    rows = params.shape[2]
    hbm = pl.BlockSpec(memory_space=pltpu.HBM)
    vmem = pl.BlockSpec(memory_space=pltpu.VMEM)
    shape = jax.ShapeDtypeStruct(params.shape, f32)
    flat = pltpu.VMEM((rows, W), f32)
    total = pltpu.VMEM((NB, rows, K), f32)
    low = pltpu.VMEM((NB, LANES, K), bf16)
    high = pltpu.VMEM((NB, CHUNKS * rows, K), f32)
    results = pl.pallas_call(
        functools.partial(kernel, n_row, n_col),
        out_shape=(flat, flat, flat, total, low, high, flat),
        in_specs=[hbm] * 5,
        out_specs=(vmem,) * 7,
        scratch_shapes=[
            pltpu.VMEM((NB, ROUNDS, K), jnp.int32),
            pltpu.VMEM((ROUNDS, W), jnp.int32),
            pltpu.VMEM((2, rows, W), f32),
            pltpu.VMEM((NB, LANES, K), bf16),
            pltpu.VMEM((NB, CHUNKS * rows, K), f32),
            pltpu.VMEM((ROUNDS, NB, rows, K), f32),
            pltpu.VMEM((ROUNDS, 4, NB, rows, K), f32),
        ] + [pltpu.VMEM((NB, rows, K), f32)] * 13 + [
            pltpu.SemaphoreType.DMA((3 + 2 * NB,)),
            pltpu.SemaphoreType.DMA((ROUNDS, 4, len(GROUPS))),
            pltpu.SemaphoreType.DMA((ROUNDS, 4, len(GROUPS))),
            pltpu.SemaphoreType.DMA((4, len(GROUPS))),
            pltpu.SemaphoreType.REGULAR,
        ],
        compiler_params=pltpu.CompilerParams(
            collective_id=0, has_side_effects=True, vmem_limit_bytes=32 * 1024 * 1024
        ),
    )(*(pltpu.with_memory_space_constraint(a, pltpu.HBM) for a in (
        params, public_copy, neighbour_mix, jnp.transpose(row_orders, (1, 0, 2)), sign_bits)))
    return pl.pallas_call(
        last_kernel,
        out_shape=(shape, shape, shape),
        in_specs=[vmem] * 7,
        out_specs=(hbm, hbm, hbm),
        scratch_shapes=[pltpu.VMEM((rows, W), f32), pltpu.VMEM((rows, W), f32), pltpu.SemaphoreType.DMA((1 + 2 * NB,))],
    )(*(pltpu.with_memory_space_constraint(a, pltpu.VMEM) for a in results))


def solution(mesh):
    split = P("row", "col", "shard", None)
    return jax.shard_map(
        functools.partial(local, mesh.shape["row"], mesh.shape["col"]),
        mesh=mesh,
        in_specs=(split, split, split, P(), P()),
        out_specs=(split, split, split),
        check_vma=False,
    )
```

```python
import functools

import jax
import jax.numpy as jnp
from jax import lax
from jax.experimental import pallas as pl
from jax.experimental.pallas import tpu as pltpu
from jax.sharding import PartitionSpec as P

W = 5120
B = 1024
K = 256
ROUNDS = 2
NB = W // B
LANES = 128
CHUNKS = B // LANES

mix_weight = 0.2
step_gamma = 0.5
decode_scale = 1.0 / K

GROUPS = ((0, 2), (2, 5))
EDGE = 8
NEXT_ROW, PREV_ROW, CHIP, SIDE = range(4)

f32 = jnp.float32
bf16 = jnp.bfloat16


def plus_minus(value, bits):
    shift = bits
    while shift > 1:
        shift = (shift + 1) // 2
        value = value ^ (value >> shift)
    return (1 - 2 * (value & 1)).astype(f32)


def rows_of(order, count):
    return plus_minus(order & lax.broadcasted_iota(jnp.int32, (count, K), 0), 4)


def low_matrix(order):
    outer, inner = rows_of((order >> 3) & 15, 16), rows_of(order & 7, 8)
    return jnp.concatenate([outer[i:i + 1] * inner for i in range(16)], axis=0).astype(bf16)


def high_signs(order, rows):
    chunk = rows_of(order >> 7, CHUNKS)
    return jnp.concatenate([jnp.broadcast_to(chunk[i:i + 1], (rows, K)) for i in range(CHUNKS)], axis=0)


def halves(value):
    top = value.astype(bf16)
    return top, (value - top.astype(f32)).astype(bf16)


def encode(diff, low, high):
    rows = diff.shape[0]
    stacked = jnp.concatenate([diff[:, c * LANES:(c + 1) * LANES] for c in range(CHUNKS)], axis=0)
    both = jnp.concatenate(halves(stacked), axis=1)
    twice = jnp.concatenate([low, low], axis=0)
    parts = high * jnp.dot(both, twice, preferred_element_type=f32)
    return jnp.sum(parts.reshape(CHUNKS, rows, K), axis=0)


def decode(code, low, high):
    rows = code.shape[0]
    spread = high * jnp.concatenate([code] * CHUNKS, axis=0)
    both = jnp.concatenate(halves(spread), axis=0)
    result = lax.dot_general(both, low, (((1,), (1,)), ((), ())), preferred_element_type=f32)
    result = result[:CHUNKS * rows] + result[CHUNKS * rows:]
    return jnp.concatenate([result[c * rows:(c + 1) * rows] for c in range(CHUNKS)], axis=1)


def kernel(n_row, n_col, x_in, h_in, s_in, order_in, bits_in, x_v, h_v, s_v,
           order_v, bits_v, sign_v, low_v, high_v, code_v, got_v,
           self_v, base_v, rows_v, cols_v, next_v, last_v, side_v, both_v, full_v,
           more_v, out_v, aside_v, back_v,
           in_sem, send_sem, recv_sem, aside_sem, ready):
    rows = x_v.shape[0]
    row, col = lax.axis_index("row"), lax.axis_index("col")
    even = lax.rem(col, 2) == 0
    odd = jnp.logical_not(even)
    chip_col = jnp.where(even, col + 1, col - 1)
    side_col = lax.rem(jnp.where(even, col + n_col - 1, col + 1), n_col)
    next_row, prev_row = lax.rem(row + 1, n_row), lax.rem(row + n_row - 1, n_row)
    neighbours = ({"row": next_row}, {"row": prev_row}, {"col": chip_col}, {"col": side_col})

    def load(i, source, target):
        return pltpu.make_async_copy(source, target, in_sem.at[i])

    order_load = load(0, order_in.at[:, :, pl.ds(0, K)], order_v)
    bits_load = load(1, bits_in, bits_v)
    x_loads = [load(2 + j, x_in.at[0, 0, :, pl.ds(j * B, B)], x_v.at[:, pl.ds(j * B, B)]) for j in range(NB)]
    h_loads = [load(2 + NB + j, h_in.at[0, 0, :, pl.ds(j * B, B)], h_v.at[:, pl.ds(j * B, B)]) for j in range(NB)]
    s_load = load(2 + 2 * NB, s_in.at[0, 0], s_v)
    edge = lax.rem(row, EDGE) == 0
    inner = jnp.logical_not(edge)
    before_edge = lax.rem(row, EDGE) == EDGE - 1
    early = jnp.where(edge, PREV_ROW, NEXT_ROW)
    late = jnp.where(edge, NEXT_ROW, PREV_ROW)
    pair = jnp.where(even, side_col, col) // 2
    middle = n_col // 4
    lopsided = jnp.logical_or(pair < middle, pair == n_col // 2 - 1)
    first_side = jnp.logical_and(lopsided, (pair < middle) == odd)
    last_side = jnp.logical_not(first_side)
    at_cut = jnp.logical_or(pair < middle, pair == n_col // 2 - 1)
    two_before = lax.rem(row, EDGE) == EDGE - 2
    aside_from = jnp.logical_and(even, jnp.logical_or(two_before, jnp.logical_and(before_edge, at_cut)))
    aside_by = jnp.logical_and(before_edge, jnp.logical_and(odd, at_cut))
    aside_to = jnp.logical_and(edge, jnp.logical_or(even, at_cut))
    at_end = pair == n_col // 2 - 1
    back_from = jnp.logical_and(before_edge, jnp.logical_and(odd, at_end))
    back_by = jnp.logical_and(edge, jnp.logical_and(odd, at_end))
    back_to = jnp.logical_and(edge, jnp.logical_and(even, at_end))
    aside_target = {
        "row": jnp.where(before_edge, next_row, lax.rem(row + 2, n_row)),
        "col": jnp.where(before_edge, side_col, col),
    }
    aside_source = {
        "row": jnp.where(odd, prev_row, lax.rem(row + n_row - 2, n_row)),
        "col": jnp.where(odd, side_col, col),
    }

    barrier = pltpu.get_barrier_semaphore()

    def greet(device):
        pl.semaphore_signal(barrier, inc=1, device_id=device, device_id_type=pl.DeviceIdType.MESH)

    pl.when(jnp.logical_or(first_side, jnp.logical_not(lopsided)))(lambda: greet(neighbours[SIDE]))
    greet(neighbours[CHIP])
    greet(neighbours[PREV_ROW])
    pl.when(jnp.logical_not(before_edge))(lambda: greet(neighbours[NEXT_ROW]))
    pl.when(aside_to)(lambda: greet(aside_source))
    pl.when(back_to)(lambda: greet({"row": prev_row, "col": side_col}))
    greetings = 1 + jnp.where(edge, 1, 2) + jnp.where(first_side, 0, 1) + jnp.where(jnp.logical_or(aside_from, back_from), 1, 0)

    for each in [order_load, bits_load] + [load for pair in zip(x_loads, h_loads) for load in pair] + [s_load]:
        each.start()

    def build(r):
        for j in range(NB):
            order = order_v[j, r:r + 1, :]
            low_v[r, j] = low_matrix(order)
            high_v[r, j] = high_signs(order, rows)

    def columns(j):
        return slice(j * B, (j + 1) * B)

    def signs(r):
        return jnp.broadcast_to((2 * bits_v[r:r + 1, :] - 1).astype(f32), (rows, W))

    def copy(r, n, g, source):
        first, last = GROUPS[g]
        part = pl.ds(first, last - first)
        return pltpu.make_async_remote_copy(
            src_ref=source.at[part],
            dst_ref=got_v.at[r, n, part],
            send_sem=send_sem.at[r, n, g],
            recv_sem=recv_sem.at[r, n, g],
            device_id=neighbours[n],
            device_id_type=pl.DeviceIdType.MESH,
        )

    def send(r, targets, g, source):
        for n in targets:
            copy(r, n, g, source).start()

    def copy_aside(g):
        first, last = GROUPS[g]
        part = pl.ds(first, last - first)
        return pltpu.make_async_remote_copy(
            src_ref=code_v.at[0, part],
            dst_ref=aside_v.at[part],
            send_sem=aside_sem.at[0, g],
            recv_sem=aside_sem.at[1, g],
            device_id=aside_target,
            device_id_type=pl.DeviceIdType.MESH,
        )

    def copy_back(g):
        first, last = GROUPS[g]
        part = pl.ds(first, last - first)
        return pltpu.make_async_remote_copy(
            src_ref=code_v.at[0, part],
            dst_ref=back_v.at[part],
            send_sem=aside_sem.at[2, g],
            recv_sem=aside_sem.at[3, g],
            device_id={"row": next_row, "col": side_col},
            device_id_type=pl.DeviceIdType.MESH,
        )

    def receive(r, sources, g):
        first, last = GROUPS[g]
        for n in sources:
            arrived = got_v.at[r, n, pl.ds(first, last - first)]
            pltpu.make_async_copy(arrived, arrived, recv_sem.at[r, n, g]).wait()

    signals = jnp.logical_and(lopsided, last_side)

    @pl.when(signals)
    def _():
        pl.semaphore_wait(barrier, greetings)
        pl.semaphore_signal(ready, inc=1, device_id=neighbours[SIDE], device_id_type=pl.DeviceIdType.MESH)

    order_load.wait()
    build(0)
    bits_load.wait()
    sign_v[0] = signs(0)
    for g, (first, last) in enumerate(GROUPS):
        for j in range(first, last):
            x_loads[j].wait()
            h_loads[j].wait()
        for j in range(first, last):
            cols = columns(j)
            code_v[0, j] = encode(sign_v[0, :, cols] * (x_v[:, cols] - h_v[:, cols]), low_v[0, j], high_v[0, j])
        if g == 0:
            pl.when(jnp.logical_not(signals))(lambda: pl.semaphore_wait(barrier, greetings))
        pl.when(aside_from)(lambda g=g: copy_aside(g).start())
        pl.when(last_side)(lambda g=g: send(0, (SIDE,), g, code_v.at[0]))
        pl.when(back_from)(lambda g=g: copy_back(g).start())
        send(0, (CHIP,), g, code_v.at[0])
        pl.when(jnp.logical_not(aside_from))(lambda g=g: send(0, (NEXT_ROW,), g, code_v.at[0]))
        pl.when(inner)(lambda g=g: send(0, (PREV_ROW,), g, code_v.at[0]))

    @pl.when(aside_from)
    def _():
        for g in range(len(GROUPS)):
            send(0, (NEXT_ROW,), g, code_v.at[0])

    build(1)
    sign_v[1] = signs(1)
    sign_v[2] = step_gamma * sign_v[0] * sign_v[1]
    left_out = jnp.where(lax.rem(row, EDGE) == 1, 0.0, 1.0)
    s_load.wait()
    for j in range(NB):
        cols = columns(j)
        decoded = decode(decode_scale * code_v[0, j], low_v[0, j], high_v[0, j])
        update = sign_v[0, :, cols] * decoded
        public = h_v[:, cols] + update
        mixed = s_v[:, cols]
        x_v[:, cols] = x_v[:, cols] - step_gamma * public
        base = x_v[:, cols] + step_gamma * mixed - public
        h_v[:, cols] = public
        s_v[:, cols] = mixed + mix_weight * update
        self_v[j] = encode(mix_weight * sign_v[2, :, cols] * decoded, low_v[1, j], high_v[1, j])
        more_v[j] = left_out * self_v[j]
        base_v[j] = encode(sign_v[1, :, cols] * base, low_v[1, j], high_v[1, j]) + self_v[j]

    twice = jnp.where(even, 0.0, 2.0)

    def part(j, code, mix=True):
        cols = columns(j)
        decoded = decode((mix_weight * decode_scale) * code, low_v[0, j], high_v[0, j])
        if mix:
            s_v[:, cols] = s_v[:, cols] + sign_v[0, :, cols] * decoded
        return encode(sign_v[2, :, cols] * decoded, low_v[1, j], high_v[1, j])

    @pl.when(jnp.logical_and(before_edge, even))
    def _():
        for g in range(len(GROUPS)):
            send(1, (NEXT_ROW,), g, base_v)

    for g in range(len(GROUPS)):
        receive(0, (CHIP,), g)
    for j in range(NB):
        cols_v[j] = part(j, got_v[0, CHIP, j])

    @pl.when(first_side)
    def _():
        pl.semaphore_wait(ready, 1)
        for g in range(len(GROUPS)):
            send(0, (SIDE,), g, code_v.at[0])

    for g in range(len(GROUPS)):
        receive(0, (early,), g)
    for j in range(NB):
        rows_v[j] = part(j, got_v[0, early, j])
        next_v[j] = base_v[j] + rows_v[j] + twice * cols_v[j]

    @pl.when(jnp.logical_or(jnp.logical_and(jnp.logical_and(inner, even), jnp.logical_not(before_edge)), aside_by))
    def _():
        for g in range(len(GROUPS)):
            send(1, (NEXT_ROW,), g, next_v)

    for g, (first, last) in enumerate(GROUPS):
        receive(0, (SIDE,), g)
        for j in range(first, last):
            side_part = part(j, got_v[0, SIDE, j])
            last_v[j] = next_v[j] + twice * side_part
            cols_v[j] = cols_v[j] + side_part
            side_v[j] = base_v[j] + cols_v[j]
            both_v[j] = side_v[j] + twice * rows_v[j]
        pl.when(jnp.logical_and(jnp.logical_and(inner, odd), jnp.logical_not(aside_by)))(
            lambda g=g: send(1, (NEXT_ROW,), g, last_v)
        )
        pl.when(even)(lambda g=g: send(1, (CHIP, SIDE), g, side_v))
        pl.when(back_by)(lambda g=g: send(1, (SIDE,), g, both_v))

    for g, (first, last) in enumerate(GROUPS):
        receive(0, (late,), g)
        for j in range(first, last):
            late_part = part(j, got_v[0, late, j])
            rows_v[j] = rows_v[j] + late_part
            code_v[1, j] = last_v[j] + late_part
            out_v[j] = side_v[j] + twice * rows_v[j]
        pl.when(jnp.logical_and(odd, jnp.logical_not(back_by)))(lambda g=g: send(1, (SIDE,), g, out_v))
        pl.when(odd)(lambda g=g: send(1, (CHIP,), g, out_v))
        pl.when(edge)(lambda g=g: send(1, (NEXT_ROW,), g, code_v.at[1]))
        send(1, (PREV_ROW,), g, code_v.at[1])
        pl.when(edge)(lambda g=g: send(0, (PREV_ROW,), g, code_v.at[0]))

    for j in range(NB):
        cols = columns(j)
        own = base_v[j] + rows_v[j] + cols_v[j]
        full_v[j] = own
        public = h_v[:, cols] + sign_v[1, :, cols] * decode(decode_scale * own, low_v[1, j], high_v[1, j])
        h_v[:, cols] = public
        x_v[:, cols] = x_v[:, cols] + step_gamma * (2 * s_v[:, cols] - public)

    @pl.when(aside_to)
    def _():
        for g in range(len(GROUPS)):
            copy_aside(g).wait_recv()
        for j in range(NB):
            more_v[j] = more_v[j] + jnp.where(odd, 2.0, 1.0) * part(j, aside_v[j], mix=False)

    @pl.when(back_to)
    def _():
        for g in range(len(GROUPS)):
            copy_back(g).wait_recv()
        for j in range(NB):
            more_v[j] = more_v[j] + 2 * part(j, back_v[j], mix=False)

    for g, (first, last) in enumerate(GROUPS):
        receive(1, range(4), g)
        for j in range(first, last):
            cols = columns(j)
            total = full_v[j] + more_v[j]
            for n in range(4):
                total = total + got_v[1, n, j]
            decoded = decode((mix_weight * decode_scale) * total, low_v[1, j], high_v[1, j])
            update = sign_v[1, :, cols] * decoded
            s_v[:, cols] = s_v[:, cols] + update
            x_v[:, cols] = x_v[:, cols] + step_gamma * update
    for r in range(ROUNDS):
        for n in range(4):
            for g in range(len(GROUPS)):
                copy(r, n, g, code_v.at[r]).wait_send()

    @pl.when(aside_from)
    def _():
        for g in range(len(GROUPS)):
            copy_aside(g).wait_send()

    @pl.when(back_from)
    def _():
        for g in range(len(GROUPS)):
            copy_back(g).wait_send()


def store_kernel(x_in, h_in, s_in, x_out, h_out, s_out, sem):
    pairs = ((x_in, x_out), (h_in, h_out), (s_in, s_out))
    copies = [pltpu.make_async_copy(a, b.at[0, 0], sem.at[i]) for i, (a, b) in enumerate(pairs)]
    for copy in copies:
        copy.start()
    for copy in copies:
        copy.wait()


def local(n_row, n_col, params, public_copy, neighbour_mix, row_orders, sign_bits):
    rows = params.shape[2]
    hbm = pl.BlockSpec(memory_space=pltpu.HBM)
    vmem = pl.BlockSpec(memory_space=pltpu.VMEM)
    shape = jax.ShapeDtypeStruct(params.shape, f32)
    flat = pltpu.VMEM((rows, W), f32)
    results = pl.pallas_call(
        functools.partial(kernel, n_row, n_col),
        out_shape=(flat, flat, flat),
        in_specs=[hbm] * 5,
        out_specs=(vmem, vmem, vmem),
        scratch_shapes=[
            pltpu.VMEM((NB, ROUNDS, K), jnp.int32),
            pltpu.VMEM((ROUNDS, W), jnp.int32),
            pltpu.VMEM((3, rows, W), f32),
            pltpu.VMEM((ROUNDS, NB, LANES, K), bf16),
            pltpu.VMEM((ROUNDS, NB, CHUNKS * rows, K), f32),
            pltpu.VMEM((ROUNDS, NB, rows, K), f32),
            pltpu.VMEM((ROUNDS, 4, NB, rows, K), f32),
        ] + [pltpu.VMEM((NB, rows, K), f32)] * 13 + [
            pltpu.SemaphoreType.DMA((3 + 2 * NB,)),
            pltpu.SemaphoreType.DMA((ROUNDS, 4, len(GROUPS))),
            pltpu.SemaphoreType.DMA((ROUNDS, 4, len(GROUPS))),
            pltpu.SemaphoreType.DMA((4, len(GROUPS))),
            pltpu.SemaphoreType.REGULAR,
        ],
        compiler_params=pltpu.CompilerParams(
            collective_id=0, has_side_effects=True, vmem_limit_bytes=32 * 1024 * 1024
        ),
    )(*(pltpu.with_memory_space_constraint(a, pltpu.HBM) for a in (
        params, public_copy, neighbour_mix, jnp.transpose(row_orders, (1, 0, 2)), sign_bits)))
    return pl.pallas_call(
        store_kernel,
        out_shape=(shape, shape, shape),
        in_specs=[vmem] * 3,
        out_specs=(hbm, hbm, hbm),
        scratch_shapes=[pltpu.SemaphoreType.DMA((3,))],
    )(*(pltpu.with_memory_space_constraint(a, pltpu.VMEM) for a in results))


def solution(mesh):
    split = P("row", "col", "shard", None)
    return jax.shard_map(
        functools.partial(local, mesh.shape["row"], mesh.shape["col"]),
        mesh=mesh,
        in_specs=(split, split, split, P(), P()),
        out_specs=(split, split, split),
        check_vma=False,
    )
```
